32 devices in a mesh: scene: 2 (over x), mrow: 8 (over z, y), mcol: 2 (over core).
Axes of the slice: x: 2, y: 2, z: 4, core: 2. Of those that a mesh axis runs over, the one named last changes fastest.
Arguments:
- pan_blocks: bfloat16 [2048, 128, 128], P(('scene', 'mrow', 'mcol')), parts along dimension 0, may hold values from -6 to 6
- ms_blocks: bfloat16 [2048, 32, 256], P(('scene', 'mrow', 'mcol')), parts along dimension 0, may hold values from -6 to 6
- send_list: int32 [3, 2048], P(None, ('scene', 'mrow', 'mcol')), parts along dimension 1, may hold values from 0 to 127, as said below
- tile_list: int32 [3, 4096], P(None, ('scene', 'mrow', 'mcol')), parts along dimension 1, may hold values from 0 to 9, as said below
- row_grid: float32 [48], P(('scene', 'mrow')), parts along dimension 0, may hold values from -32 to 288
- col_grid: float32 [16, 16], P(('scene', 'mrow'), 'mcol'), parts along dimension 0, may hold values from -32 to 1312
- band_mix: float32 [8, 8], replicated, may hold values from -1.5 to 1.5
- band_gain: float32 [8], replicated, may hold values from 0.4 to 1.2
- synth_weight: float32 [8], replicated, may hold values from 0.05 to 0.3
Outputs:
- sharpened: bfloat16 [8, 2048, 1024], P(None, ('scene', 'mrow'), 'mcol'), parts along dimension 1
The draws below stay inside these ranges and needn't reach their ends.
There are 2 independent parts, one for each index of `scene`. The reference program is written for one: setup_inputs(seed, part) draws one part's arguments, and reference() takes and returns one part's arrays. A program takes and returns all parts, laid end to end along the dimension named above; an argument that names none is the same for every part. Nothing has to cross between parts.
Inputs may be any that keep to these rules, and one draw needn't show every extreme that they name: `send_list`: row 0 gives each source block of a device a distinct send slot; slot p goes to map-row owner p // 16 in the device's own map column, so one device sends at most 16 blocks to one tile; in every draw one tile of each map column receives 16 blocks from every device of that column, and every device fills 16 slots of it. Row 1 is a cell row below 2; row 2 a cell column between mcol * 5 and mcol * 5 + 4. `tile_list`: row 0 is 1 exactly in the receive slots that send_list fills and 0 elsewhere; rows 1 and 2 repeat the cell row and column of the block sent there, and are 0 in empty slots.
All inputs are finite; a program needn't handle non-finite values.
Results may differ from the reference program's by a relative error of at most 0.0073.
Values may be sent and summed in bfloat16 or wider, within the bound.
No kernel may reach another device: no remote copies, remote signals or barrier semaphores. Data moves between devices by JAX's collectives and lax.ppermute only.
A program may use at most 128 MiB of HBM per device.

```python
import math
import jax
import jax.numpy as jnp
from jax import lax

BANDS = 8
BS = 128
GRID = 64
TR = 128
TC = 512
SBD = 64
MB = 32
KR = 2
KC = 5
NR = 1024
NC = 1024
N_MROW = 8
N_MCOL = 2


def route_tables(key):
    devices = N_MROW * N_MCOL
    partition_total = 2 * SBD
    capacity = partition_total // N_MROW
    stochastic_seed_sequence = jax.random.split(jax.random.fold_in(key, 4242), 6)
    favoured = jax.random.randint(stochastic_seed_sequence[0], (N_MCOL,), 0, N_MROW)
    preference_extra_digits = jax.random.randint(stochastic_seed_sequence[1], (N_MCOL, N_MROW), 0, 4)
    stochastic_perturb_digits = jax.random.randint(stochastic_seed_sequence[2], (devices, partition_total), 0, 1024)
    partition_number = jnp.arange(partition_total, dtype=jnp.int32)
    keeper_line = partition_number // capacity
    horizontal_location = jnp.arange(devices, dtype=jnp.int32) % N_MCOL
    reached_capacity_flag = (keeper_line[None, :] == jnp.take(favoured, horizontal_location)[:, None]).astype(jnp.int32)
    preference_extra_order = jnp.take(jnp.take(preference_extra_digits, horizontal_location, axis=0), keeper_line, axis=1)
    preference_grades = ((reached_capacity_flag * 8 + preference_extra_order) * 1024 + stochastic_perturb_digits) * partition_total + partition_number[None, :]
    top_scores, chosen = lax.top_k(preference_grades, SBD)
    shuffle = jax.random.randint(stochastic_seed_sequence[5], (devices, SBD), 0, 4096) * SBD + jnp.arange(SBD, dtype=jnp.int32)[None, :]
    reorder = jnp.argsort(shuffle, axis=1)
    chosen = jnp.take_along_axis(chosen, reorder, axis=1).astype(jnp.int32)
    cell_rows = jax.random.randint(stochastic_seed_sequence[3], (devices, SBD), 0, KR)
    cell_cols = horizontal_location[:, None] * KC + jax.random.randint(stochastic_seed_sequence[4], (devices, SBD), 0, KC)
    flat_slots = chosen.reshape(-1)
    sender = jnp.repeat(jnp.arange(devices, dtype=jnp.int32), SBD)
    destination = (flat_slots // capacity * N_MCOL + sender % N_MCOL) * partition_total + sender // N_MCOL * capacity + flat_slots % capacity
    entries = jnp.stack([jnp.ones_like(flat_slots), cell_rows.reshape(-1), cell_cols.reshape(-1)]).astype(jnp.int32)
    tile_table = jnp.zeros((3, devices * partition_total), jnp.int32).at[:, destination].set(entries)
    send_table = jnp.stack([flat_slots, cell_rows.reshape(-1), cell_cols.reshape(-1)]).astype(jnp.int32)
    return (send_table, tile_table)


def draw_send_list(key, part):
    return route_tables(key)[0]


def draw_tile_list(key, part):
    return route_tables(key)[1]


def draw_row_grid(key, part):
    node_count = TR // GRID + 1
    stochastic_seed_sequence = jax.random.split(jax.random.fold_in(key, 11), 3)
    reach = float(KR * BS)
    lead_gap = jax.random.uniform(stochastic_seed_sequence[0], (N_MROW, 1), minval=1.0, maxval=6.0)
    tail_gap = jax.random.uniform(stochastic_seed_sequence[1], (N_MROW, 1), minval=1.0, maxval=6.0)
    shake = 0.15
    fraction = jnp.arange(node_count, dtype=jnp.int32).astype(jnp.float32) / (node_count - 1)
    jitter = jax.random.uniform(stochastic_seed_sequence[2], (N_MROW, node_count), minval=-1.0, maxval=1.0) * (shake * GRID)
    nodes_all = lead_gap + (reach - lead_gap - tail_gap) * fraction[None, :] + jitter
    return nodes_all.reshape(-1).astype(jnp.float32)


def draw_col_grid(key, part):
    node_count = NC // GRID
    stochastic_seed_sequence = jax.random.split(jax.random.fold_in(key, 23), 3)
    reach = float(N_MCOL * KC * BS)
    lead_gap = jax.random.uniform(stochastic_seed_sequence[0], (N_MROW, 1), minval=1.0, maxval=6.0)
    tail_gap = jax.random.uniform(stochastic_seed_sequence[1], (N_MROW, 1), minval=1.0, maxval=6.0)
    shake = 0.15
    fraction = (GRID * jnp.arange(node_count, dtype=jnp.int32)).astype(jnp.float32) / NC
    jitter = jax.random.uniform(stochastic_seed_sequence[2], (N_MROW, node_count), minval=-1.0, maxval=1.0) * (shake * GRID)
    return (lead_gap + (reach - lead_gap - tail_gap) * fraction[None, :] + jitter).astype(jnp.float32)


def shard_levels(own_key, extent, shards, smallest, high):
    gain = 1.0
    for dim, shards_of in shards:
        heights = jax.random.uniform(jax.random.fold_in(jax.random.fold_in(own_key, 6), dim), (shards_of,), jnp.float32, smallest / len(shards), high / len(shards))
        gain = gain * jnp.repeat(jnp.exp(heights), extent[dim] // shards_of).reshape((-1,) + (1,) * (len(extent) - 1 - dim))
    return gain


def bell_draw(stream_key, shape, spread, most, pieces=(), kind=jnp.bfloat16):
    values = jax.random.normal(stream_key, shape, jnp.float32) * spread
    if len(pieces) > 0:
        values = shard_levels(stream_key, shape, pieces, -0.22, 0.18) * values
    return jnp.clip(values, min=-most, max=most).astype(kind)


def setup_inputs(seed: int = 0, part: int = 0) -> dict:
    streams_of = jax.random.split(jax.random.key(seed), 10)
    part_splits = jax.random.split(jax.random.fold_in(streams_of[9], part), 10)
    return {
        "pan_blocks": bell_draw(part_splits[0], (N_MROW * N_MCOL * SBD, BS, BS), 1.0, 6.0, ((0, 16),)),
        "ms_blocks": bell_draw(part_splits[1], (N_MROW * N_MCOL * SBD, MB, BANDS * MB), 1.0, 6.0, ((0, 16),)),
        "send_list": draw_send_list(jax.random.fold_in(jax.random.fold_in(streams_of[9], part), 71), part),
        "tile_list": draw_tile_list(jax.random.fold_in(jax.random.fold_in(streams_of[9], part), 71), part),
        "row_grid": draw_row_grid(jax.random.fold_in(jax.random.fold_in(streams_of[9], part), 71), part),
        "col_grid": draw_col_grid(jax.random.fold_in(jax.random.fold_in(streams_of[9], part), 71), part),
        "band_mix": bell_draw(streams_of[6], (BANDS, BANDS), 0.3, 1.5, (), jnp.float32),
        "band_gain": jnp.clip(jax.random.uniform(streams_of[7], (BANDS,), jnp.float32, 0.4, 1.2), 0.4, 1.2),
        "synth_weight": jnp.clip(jnp.exp(jax.random.uniform(streams_of[8], (BANDS,), jnp.float32, math.log(0.05), math.log(0.3))), 0.05, 0.3),
    }


highest = lax.Precision.HIGHEST


def cubic_weight(offset):
    distance = jnp.abs(offset)
    near_part = (1.5 * distance - 2.5) * distance * distance + 1.0
    far_part = ((-0.5 * distance + 2.5) * distance - 4.0) * distance + 2.0
    return jnp.where(distance <= 1.0, near_part, jnp.where(distance < 2.0, far_part, jnp.zeros_like(distance)))


def along_nodes(node_values, position, offset, spacing):
    segment = jnp.minimum(position // spacing, node_values.shape[-1] - 2)
    left_node = jnp.take(node_values, segment, axis=-1)
    right_node = jnp.take(node_values, segment + 1, axis=-1)
    within = ((position - segment * spacing).astype(jnp.float32) + offset) / spacing
    return left_node + (right_node - left_node) * within


def source_weights(coords, cell_ids, block_size):
    pixels = (cell_ids[:, None, None] * block_size + jnp.arange(block_size, dtype=jnp.int32)[None, None, :]).astype(jnp.float32)
    return cubic_weight(coords[:, :, None] - pixels).astype(jnp.bfloat16)


def row_weights(coords, cell_ids, is_valid, block_size):
    pixels = (cell_ids[None, :, None] * block_size + jnp.arange(block_size, dtype=jnp.int32)[None, None, :]).astype(jnp.float32)
    return (cubic_weight(coords[:, None, None] - pixels) * is_valid[None, :, None]).astype(jnp.bfloat16)


def upsample_table(length, coarse):
    position = (jnp.arange(length, dtype=jnp.int32).astype(jnp.float32) - 1.5) * 0.25 + 2.0
    taps = jnp.arange(coarse + 4, dtype=jnp.int32).astype(jnp.float32)
    return cubic_weight(position[:, None] - taps[None, :]).astype(jnp.bfloat16)


def combine(upsampled, pan_map, band_mix, band_gain, synth_weight):
    mixture = jnp.transpose(upsampled, (1, 0, 2)) + jnp.einsum("bk,rkc->brc", band_mix, upsampled, precision=highest)
    synthetic = jnp.einsum("k,rkc->rc", synth_weight, upsampled, precision=highest)
    return (mixture + band_gain[:, None, None] * (pan_map - synthetic)[None, :, :]).astype(jnp.bfloat16)


def reference(pan_blocks, ms_blocks, send_list, tile_list, row_grid, col_grid, band_mix, band_gain, synth_weight):
    devices = N_MROW * N_MCOL
    partition_total = 2 * SBD
    capacity = partition_total // N_MROW
    node_count = TR // GRID + 1
    coarse_rows = TR // 4
    coarse_cols = TC // 4
    block_ids = jnp.arange(devices * SBD, dtype=jnp.int32)
    sender = block_ids // SBD
    partition_number = send_list[0]
    target = ((partition_number // capacity) * N_MCOL + sender % N_MCOL) * partition_total + (sender // N_MCOL) * capacity + partition_number % capacity
    receive = jnp.zeros((devices * partition_total,), jnp.int32).at[target].set(block_ids)

    def one_tile(device):
        row_band = device // N_MCOL
        horizontal_location = device % N_MCOL
        slot_index = lax.dynamic_slice_in_dim(receive, device * partition_total, partition_total)
        tile_lists = lax.dynamic_slice_in_dim(tile_list, device * partition_total, partition_total, 1)
        is_valid = tile_lists[0].astype(jnp.float32)
        cell_rows = tile_lists[1]
        cell_cols = tile_lists[2]
        pan_data = jnp.take(pan_blocks, slot_index, axis=0).astype(jnp.float32)
        ms_data = jnp.take(ms_blocks, slot_index, axis=0).astype(jnp.float32).reshape(partition_total, MB, BANDS, MB)
        row_nodes = lax.dynamic_slice_in_dim(row_grid, row_band * node_count, node_count)
        col_nodes = lax.dynamic_index_in_dim(col_grid, row_band, 0, False)
        map_rows = jnp.arange(TR, dtype=jnp.int32)
        map_cols = horizontal_location * TC + jnp.arange(TC, dtype=jnp.int32)
        y_pan = along_nodes(row_nodes, map_rows, 0.0, GRID)
        x_pan = along_nodes(col_nodes, map_cols, 0.0, GRID)
        y_ms = (along_nodes(row_nodes, 4 * jnp.arange(coarse_rows, dtype=jnp.int32) + 1, 0.5, GRID) - 1.5) * 0.25
        x_ms = (along_nodes(col_nodes, horizontal_location * TC + 4 * jnp.arange(coarse_cols, dtype=jnp.int32) + 1, 0.5, GRID) - 1.5) * 0.25
        col_weight = source_weights(x_pan[None, :], cell_cols, BS)
        pan_cols = jnp.einsum("sij,scj->sic", pan_data, col_weight.astype(jnp.float32), precision=highest).astype(jnp.bfloat16)
        row_weight = row_weights(y_pan, cell_rows, is_valid, BS)
        pan_map = jnp.dot(row_weight.reshape(TR, partition_total * BS), pan_cols.reshape(partition_total * BS, TC), preferred_element_type=jnp.float32)
        ms_col_weight = source_weights(x_ms[None, :], cell_cols, MB)
        ms_cols = jnp.einsum("sibj,scj->sibc", ms_data, ms_col_weight.astype(jnp.float32), precision=highest).astype(jnp.bfloat16)
        ms_row_weight = row_weights(y_ms, cell_rows, is_valid, MB)
        ms_map = jnp.dot(ms_row_weight.reshape(coarse_rows, partition_total * MB), ms_cols.reshape(partition_total * MB, BANDS * coarse_cols), preferred_element_type=jnp.float32).astype(jnp.bfloat16)
        return pan_map, ms_map.reshape(coarse_rows, BANDS, coarse_cols)

    pan_maps, ms_maps = lax.map(one_tile, jnp.arange(devices, dtype=jnp.int32))
    strip_map = ms_maps.reshape(N_MROW, N_MCOL, coarse_rows, BANDS, coarse_cols).transpose(0, 2, 3, 1, 4).reshape(N_MROW * coarse_rows, BANDS, N_MCOL * coarse_cols)
    padded = jnp.pad(strip_map, ((2, 2), (0, 0), (2, 2)))
    up_rows = upsample_table(TR, coarse_rows)
    up_cols = upsample_table(TC, coarse_cols)

    def sharpen(device):
        row_band = device // N_MCOL
        horizontal_location = device % N_MCOL
        window = lax.dynamic_slice(padded, (row_band * coarse_rows, jnp.zeros((), jnp.int32), horizontal_location * coarse_cols), (coarse_rows + 4, BANDS, coarse_cols + 4))
        across = jnp.einsum("mbn,cn->mbc", window.astype(jnp.float32), up_cols.astype(jnp.float32), precision=highest).astype(jnp.bfloat16)
        upsampled = jnp.dot(up_rows, across.reshape(coarse_rows + 4, BANDS * TC), preferred_element_type=jnp.float32).reshape(TR, BANDS, TC)
        pan_map = lax.dynamic_index_in_dim(pan_maps, device, 0, False)
        return combine(upsampled, pan_map, band_mix, band_gain, synth_weight)

    tiles = lax.map(sharpen, jnp.arange(devices, dtype=jnp.int32))
    return tiles.reshape(N_MROW, N_MCOL, BANDS, TR, TC).transpose(2, 0, 3, 1, 4).reshape(BANDS, NR, NC)
```

```python
import functools

import jax
import jax.numpy as jnp
from jax import lax
from jax.experimental import pallas as pl
from jax.experimental.pallas import tpu as pltpu
from jax.sharding import PartitionSpec as P

GRID = 64
TR = 128
TC = 512
KR = 2
KC = 5

F32 = jnp.float32
BF16 = jnp.bfloat16
VMEM_LIMIT = 56 * 1024 * 1024


def params():
    return pltpu.CompilerParams(vmem_limit_bytes=VMEM_LIMIT)


def whole(memory_space=pltpu.VMEM):
    return pl.BlockSpec(memory_space=memory_space)


def cubic_weight(offset):
    distance = jnp.abs(offset)
    near_part = (1.5 * distance - 2.5) * distance * distance + 1.0
    far_part = ((-0.5 * distance + 2.5) * distance - 4.0) * distance + 2.0
    return jnp.where(
        distance <= 1.0, near_part, jnp.where(distance < 2.0, far_part, jnp.zeros_like(distance))
    )


def iota(shape, dim):
    return lax.broadcasted_iota(jnp.int32, shape, dim)


def along(node, local, position, offset, first, count, last):
    left = jnp.zeros(position.shape, F32)
    right = left
    start = jnp.zeros(position.shape, jnp.int32)
    for k in range(count):
        segment = jnp.minimum(first + k, last)
        here = local == k
        left = jnp.where(here, node(segment), left)
        right = jnp.where(here, node(segment + 1), right)
        start = jnp.where(here, segment * GRID, start)
    within = ((position - start).astype(F32) + offset) / GRID
    return left + (right - left) * within


def cell_sums(n_dest, group, capacity, list_ref, pan_ref, ms_ref, pan_out, ms_out, pan_acc, ms_acc):
    first = pl.program_id(0) * group
    block, coarse = pan_ref.shape[1], ms_ref.shape[1]
    pan_acc[...] = jnp.zeros_like(pan_acc)
    ms_acc[...] = jnp.zeros_like(ms_acc)

    def add(j, carry):
        place = list_ref[0, j] // capacity - first
        row, col = list_ref[1, j], list_ref[2, j]
        cell = place * KC + lax.rem(col, KC)

        @pl.when((place >= 0) & (place < group))
        def _():
            rows = pl.ds(pl.multiple_of(row * block, block), block)
            pan_acc[cell, rows, :] += pan_ref[j].astype(F32)
            rows = pl.ds(pl.multiple_of(row * coarse, coarse), coarse)
            ms_acc[cell, rows, :] += ms_ref[j].astype(F32)

        return carry

    lax.fori_loop(0, pan_ref.shape[0], add, 0)
    pan_out[...] = pan_acc[...].astype(BF16)
    ms_out[...] = ms_acc[...].astype(BF16)


def tap_fill(table, row0, rows, x, first_pixel, cols=None):
    floor = jnp.floor(x)
    taps = [cubic_weight(x - (floor - 1.0 + a)).astype(BF16) for a in range(4)]
    offset = jnp.clip(floor - 1.0 - first_pixel, -8.0, rows + 8.0)
    base = (iota(x.shape, 0).astype(F32) - offset).astype(BF16)
    zero = jnp.zeros(x.shape, BF16)
    for slab in range(rows // 16):
        value = zero
        for a in range(4):
            value = jnp.where(base == jnp.asarray(a - 16 * slab, BF16), taps[a], value)
        yield slab, value


def maps(n, bands, who, rows_ref, cols_ref, pan_ref, ms_ref, *rest):
    outs, (table, spread, edge) = rest[:n], rest[n:]
    g = pl.program_id(0)
    me, c = who[0], who[1]
    dest = me ^ g
    block = pan_ref.shape[2] // KR
    coarse = ms_ref.shape[2] // KR
    half = 128 // coarse
    halves = bands // half
    crows, ccols = TR // 4, TC // 4
    row_nodes = TR // GRID + 1
    col_nodes = cols_ref.shape[1]

    @pl.when(g == 0)
    def _():
        spread[...] = jnp.zeros_like(spread)

    def row_node(s):
        return rows_ref[g, s]

    position = iota((TR, 128), 0)
    y = along(row_node, position // GRID, position, 0.0, 0, row_nodes - 1, row_nodes - 2)
    lane = iota((TR, 128), 1)
    weight = [
        cubic_weight(y - (lane + k * 128).astype(F32)).astype(BF16)
        for k in range(KR * block // 128)
    ]
    weight = jnp.concatenate(weight, axis=1)
    source = jnp.concatenate([pan_ref[0, k] for k in range(KC)], axis=1)
    held = jnp.dot(weight, source, preferred_element_type=F32).astype(BF16)

    def col_node(s):
        return cols_ref[g, s]

    segments = TC // GRID
    local = iota((16, TC), 1)
    x = along(
        col_node, local // GRID, c * TC + local, 0.0, c * segments, segments, col_nodes - 2
    )
    for k in range(KC):
        pixel = ((c * KC + k) * block).astype(F32)
        for slab, value in tap_fill(table, k * block, block, x, pixel):
            table[pl.ds(k * block + 16 * slab, 16), :] = value
    pan_map = jnp.dot(held, table[...], preferred_element_type=F32).astype(BF16)

    i = iota((crows + 8, KR * coarse), 0)
    extra = (i - crows) % 4
    i = jnp.where(i < crows, i, jnp.where(extra < 2, crows - 2 + extra, extra - 2))
    position = 4 * i + 1
    y = along(row_node, position // GRID, position, 0.5, 0, row_nodes - 1, row_nodes - 2)
    y = (y - 1.5) * 0.25
    weight = cubic_weight(y - iota(y.shape, 1).astype(F32)).astype(BF16)
    source = jnp.concatenate([ms_ref[0, k] for k in range(KC)], axis=1)
    held = jnp.dot(weight, source, preferred_element_type=F32)
    lanes = bands * coarse
    left = jnp.concatenate(
        [
            jnp.concatenate(
                [held[:, k * lanes + h * 128 : k * lanes + h * 128 + 128] for k in range(KC)],
                axis=1,
            )
            for h in range(halves)
        ],
        axis=0,
    ).astype(BF16)
    v = iota((16, ccols), 1)
    position = 4 * v + 1
    x = along(
        col_node, position // GRID, c * TC + position, 0.5, c * segments, segments, col_nodes - 2
    )
    x = (x - 1.5) * 0.25
    for k in range(KC):
        pixel = ((c * KC + k) * coarse).astype(F32)
        for slab, value in tap_fill(spread, k * 128, coarse, x, pixel):
            for s in range(half):
                at = k * 128 + s * coarse + 16 * slab
                spread[pl.ds(at, 16), s * ccols : (s + 1) * ccols] = value
    ms_map = jnp.dot(left, spread[...], preferred_element_type=F32)
    tall = crows + 8
    main = jnp.concatenate([ms_map[h * tall : h * tall + crows] for h in range(halves)], axis=0)
    main = main.astype(BF16)
    group = ms_map[crows:tall]
    upper = iota(group.shape, 0) < 4
    edge[dest + 1] = jnp.where(upper, group, ms_map[tall + crows : 2 * tall])
    base = TR + halves * crows
    for k in range(n):

        @pl.when(g == k)
        def _(k=k):
            outs[k][0:TR, :] = pan_map
            outs[k][TR:base, :] = main

    @pl.when(g == n - 1)
    def _():
        edge[0] = jnp.zeros(edge.shape[1:], F32)
        edge[n + 1] = jnp.zeros(edge.shape[1:], F32)
        mine = (iota(group.shape, 0) & 2) == 0
        for k in range(n):
            at = me ^ k
            halo = jnp.where(mine, edge[at], edge[at + 2])
            halo = jnp.concatenate([halo, jnp.zeros_like(halo)], axis=0)
            outs[k][base : base + 16, :] = halo.astype(BF16)


def ms_total(start, *refs):
    out = refs[-1]
    total = refs[0][start:, :].astype(F32)
    for ref in refs[1:-1]:
        total = total + ref[start:, :].astype(F32)
    out[...] = total.astype(BF16)


def pan_total(stop, *refs):
    out = refs[-1]
    total = refs[0][:stop, :].astype(F32)
    for ref in refs[1:-1]:
        total = total + ref[:stop, :].astype(F32)
    out[...] = total


def tables(bands, who, mix, gain, synth, up_out, cols_out):
    c = who[1]
    crows, ccols = TR // 4, TC // 4
    half = bands // 2
    v = iota((2 * ccols, TC), 1).astype(F32)
    q = iota((2 * ccols, TC), 0)
    q = jnp.where(q < ccols, q, jnp.where(c == 0, q, q - 2 * ccols)).astype(F32)
    cols_out[...] = cubic_weight((v - 1.5) * 0.25 - q).astype(BF16)
    lanes = up_out.shape[2]
    lane = iota((1, lanes), 1)
    s = lane // 80
    q = lane - s * 80
    e = q - 2 * crows
    low = q < 2 * crows
    h = jnp.where(low, q // crows, e // 4)
    band = jnp.where((s < half) & (q < 2 * crows + 8), h * half + s, -1)
    tail = e % 4
    w = jnp.where(low, 2 + q % crows, jnp.where(tail < 2, tail, crows + tail))
    r = iota((TR, lanes), 0).astype(F32)
    up = cubic_weight((r - 1.5) * 0.25 + 2.0 - w.astype(F32)).astype(BF16).astype(F32)
    for b in range(bands):
        factor = jnp.zeros((1, lanes), F32)
        for k in range(bands):
            value = mix[b, k] - gain[b] * synth[k]
            if k == b:
                value = value + 1.0
            factor = jnp.where(band == k, value, factor)
        up_out[b] = (up * factor).astype(BF16)


def finish(bands, gain, up_ref, cols_ref, pan_ref, ms_ref, other_ref, out):
    half = bands // 2
    ccols = TC // 4
    pieces = []
    for s in range(half):
        at = slice(s * ccols, (s + 1) * ccols)
        pieces.append(jnp.concatenate([ms_ref[:, at], other_ref[:, at]], axis=1))
    left = jnp.concatenate(pieces, axis=0)
    across = jnp.dot(left, cols_ref[...], preferred_element_type=F32).astype(BF16)
    pad = up_ref.shape[2] - across.shape[0]
    if pad:
        across = jnp.concatenate([across, jnp.zeros((pad, TC), BF16)], axis=0)
    for b in range(bands):
        value = jnp.dot(up_ref[b], across, preferred_element_type=F32)
        out[b] = (value + gain[b] * pan_ref[...]).astype(BF16)


def exchange(x, step, count):
    return lax.ppermute(x, "mrow", [(i, i ^ step) for i in range(count)])


def local(
    pan_blocks,
    ms_blocks,
    send_list,
    tile_list,
    row_grid,
    col_grid,
    band_mix,
    band_gain,
    synth_weight,
):
    n = lax.axis_size("mrow")
    me, c = lax.axis_index("mrow"), lax.axis_index("mcol")
    capacity = tile_list.shape[1] // n
    own, block = pan_blocks.shape[0], pan_blocks.shape[1]
    coarse = ms_blocks.shape[1]
    bands = band_gain.shape[0]
    who = jnp.stack([me, c]).astype(jnp.int32)

    across_cols = lax.all_gather(col_grid[0], "mcol", axis=0, tiled=True)
    mine = jnp.concatenate([row_grid, across_cols])[None]
    pair = jnp.concatenate([mine, exchange(mine, 1, n)], axis=0)
    grids = jnp.concatenate([pair] + [exchange(pair, k, n) for k in range(2, n, 2)], axis=0)
    rows_all, cols_all = grids[:, : row_grid.shape[0]], grids[:, row_grid.shape[0] :]

    group = min(n, 8)
    pan_cells, ms_cells = pl.pallas_call(
        functools.partial(cell_sums, n, group, capacity),
        grid=(n // group,),
        in_specs=[whole(pltpu.SMEM), whole(), whole()],
        out_specs=[
            pl.BlockSpec((group * KC, KR * block, block), lambda i: (i, 0, 0)),
            pl.BlockSpec((group * KC, KR * coarse, bands * coarse), lambda i: (i, 0, 0)),
        ],
        out_shape=[
            jax.ShapeDtypeStruct((n * KC, KR * block, block), BF16),
            jax.ShapeDtypeStruct((n * KC, KR * coarse, bands * coarse), BF16),
        ],
        scratch_shapes=[
            pltpu.VMEM((group * KC, KR * block, block), F32),
            pltpu.VMEM((group * KC, KR * coarse, bands * coarse), F32),
        ],
        compiler_params=params(),
        name="cell_sums",
    )(send_list, pan_blocks, ms_blocks)

    start = TR
    height = TR + 2 * (TR // 4) + 16
    pieces = pl.pallas_call(
        functools.partial(maps, n, bands),
        grid_spec=pltpu.PrefetchScalarGridSpec(
            num_scalar_prefetch=3,
            grid=(n,),
            in_specs=[
                pl.BlockSpec((1, KC, KR * block, block), lambda g, w, a, b: (w[0] ^ g, 0, 0, 0)),
                pl.BlockSpec(
                    (1, KC, KR * coarse, bands * coarse), lambda g, w, a, b: (w[0] ^ g, 0, 0, 0)
                ),
            ],
            out_specs=[pl.BlockSpec((height, TC), lambda g, w, a, b: (0, 0)) for _ in range(n)],
            scratch_shapes=[
                pltpu.VMEM((KC * block, TC), BF16),
                pltpu.VMEM((KC * 128, TC), BF16),
                pltpu.VMEM((n + 2, 8, TC), F32),
            ],
        ),
        out_shape=[jax.ShapeDtypeStruct((height, TC), BF16) for _ in range(n)],
        compiler_params=params(),
        name="maps",
    )(
        who,
        rows_all,
        cols_all,
        pan_cells.reshape(n, KC, KR * block, block),
        ms_cells.reshape(n, KC, KR * coarse, bands * coarse),
    )
    got = [pieces[0]] + [exchange(pieces[k], k, n) for k in range(1, n)]

    lanes = 3 * 128
    up, cols = pl.pallas_call(
        functools.partial(tables, bands),
        in_specs=[whole(pltpu.SMEM)] * 4,
        out_specs=[whole(), whole()],
        out_shape=[
            jax.ShapeDtypeStruct((bands, TR, lanes), BF16),
            jax.ShapeDtypeStruct((TC // 2, TC), BF16),
        ],
        compiler_params=params(),
        name="tables",
    )(who, band_mix, band_gain, synth_weight)

    ms_map = pl.pallas_call(
        functools.partial(ms_total, start),
        in_specs=[whole()] * n,
        out_specs=whole(),
        out_shape=jax.ShapeDtypeStruct((height - start, TC), BF16),
        compiler_params=params(),
        name="ms_total",
    )(*got)
    other = lax.ppermute(ms_map, "mcol", [(0, 1), (1, 0)])
    pan_map = pl.pallas_call(
        functools.partial(pan_total, start),
        in_specs=[whole()] * n,
        out_specs=whole(),
        out_shape=jax.ShapeDtypeStruct((TR, TC), F32),
        compiler_params=params(),
        name="pan_total",
    )(*got)
    return pl.pallas_call(
        functools.partial(finish, bands),
        in_specs=[whole(pltpu.SMEM)] + [whole()] * 5,
        out_specs=whole(),
        out_shape=jax.ShapeDtypeStruct((bands, TR, TC), BF16),
        compiler_params=params(),
        name="finish",
    )(band_gain, up, cols, pan_map, ms_map, other)


def solution(mesh):
    return jax.shard_map(
        local,
        mesh=mesh,
        in_specs=(
            P(("scene", "mrow", "mcol"), None, None),
            P(("scene", "mrow", "mcol"), None, None),
            P(None, ("scene", "mrow", "mcol")),
            P(None, ("scene", "mrow", "mcol")),
            P(("scene", "mrow")),
            P(("scene", "mrow"), "mcol"),
            P(),
            P(),
            P(),
        ),
        out_specs=P(None, ("scene", "mrow"), "mcol"),
        check_vma=False,
    )
```

```python
import functools

import jax
import jax.numpy as jnp
from jax import lax
from jax.experimental import pallas as pl
from jax.experimental.pallas import tpu as pltpu
from jax.sharding import PartitionSpec as P

GRID = 64
TR = 128
TC = 512
KR = 2
KC = 5

F32 = jnp.float32
BF16 = jnp.bfloat16
VMEM_LIMIT = 56 * 1024 * 1024


def params():
    return pltpu.CompilerParams(vmem_limit_bytes=VMEM_LIMIT)


def whole(memory_space=pltpu.VMEM):
    return pl.BlockSpec(memory_space=memory_space)


def cubic_weight(offset):
    distance = jnp.abs(offset)
    near_part = (1.5 * distance - 2.5) * distance * distance + 1.0
    far_part = ((-0.5 * distance + 2.5) * distance - 4.0) * distance + 2.0
    return jnp.where(
        distance <= 1.0, near_part, jnp.where(distance < 2.0, far_part, jnp.zeros_like(distance))
    )


def iota(shape, dim):
    return lax.broadcasted_iota(jnp.int32, shape, dim)


def along(node, local, position, offset, first, count, last):
    left = jnp.zeros(position.shape, F32)
    right = left
    start = jnp.zeros(position.shape, jnp.int32)
    for k in range(count):
        segment = jnp.minimum(first + k, last)
        here = local == k
        left = jnp.where(here, node(segment), left)
        right = jnp.where(here, node(segment + 1), right)
        start = jnp.where(here, segment * GRID, start)
    within = ((position - start).astype(F32) + offset) / GRID
    return left + (right - left) * within


def cell_sums(group, capacity, who, list_ref, pan_ref, ms_ref, pan_out, ms_out, pan_acc, ms_acc):
    first = pl.program_id(0) * group
    block, coarse = pan_ref.shape[1], ms_ref.shape[1]
    pan_acc[...] = jnp.zeros_like(pan_acc)
    ms_acc[...] = jnp.zeros_like(ms_acc)

    def add(j, carry):
        place = ((list_ref[0, j] // capacity) ^ who[0]) - first
        row, col = list_ref[1, j], list_ref[2, j]
        cell = place * KC + lax.rem(col, KC)

        @pl.when((place >= 0) & (place < group))
        def _():
            rows = pl.ds(pl.multiple_of(row * block, block), block)
            pan_acc[cell, rows, :] += pan_ref[j].astype(F32)
            rows = pl.ds(pl.multiple_of(row * coarse, coarse), coarse)
            ms_acc[cell, rows, :] += ms_ref[j].astype(F32)

        return carry

    lax.fori_loop(0, pan_ref.shape[0], add, 0)
    pan_out[...] = pan_acc[...].astype(BF16)
    ms_out[...] = ms_acc[...].astype(BF16)


def repeat_rows(x):
    return jnp.concatenate([x, x], axis=0)


def tap_fill(rows, x, first_pixel):
    floor = jnp.floor(x)
    taps = [repeat_rows(cubic_weight(x - (floor - 1.0 + a))).astype(BF16) for a in range(4)]
    row = iota((16, x.shape[1]), 0).astype(F32)
    zero = jnp.zeros(row.shape, BF16)
    corner = floor - 1.0

    def at(first):
        offset = jnp.clip(corner - first, -8.0, rows + 8.0)
        base = (row - repeat_rows(offset)).astype(BF16)
        for slab in range(rows // 16):
            value = zero
            for a in range(4):
                value = jnp.where(base == jnp.asarray(a - 16 * slab, BF16), taps[a], value)
            yield slab, value

    for k, first in enumerate(first_pixel):
        for slab, value in at(first):
            yield k, slab, value


def row_nodes(grids, g):
    return lambda s: grids[g, s]


def col_nodes(grids, g, c):
    first = TR // GRID + 1
    each = (grids.shape[1] - first) // 2

    def node(s):
        half = s // each
        return grids[g, first + (half ^ c) * each + (s - half * each)]

    return node


def last_col(grids):
    return grids.shape[1] - (TR // GRID + 1) - 2


def ms_piece(bands, c, g, grids, cells, spread):
    coarse = cells.shape[1] // KR
    half = 128 // coarse
    halves = bands // half
    crows, ccols = TR // 4, TC // 4
    tall = crows + 8
    lanes = bands * coarse
    i = iota((tall, KR * coarse), 0)
    extra = (i - crows) % 4
    i = jnp.where(i < crows, i, jnp.where(extra < 2, crows - 2 + extra, extra - 2))
    position = 4 * i + 1
    y = along(row_nodes(grids, g), position // GRID, position, 0.5, 0, TR // GRID, TR // GRID - 1)
    y = (y - 1.5) * 0.25
    weight = cubic_weight(y - iota(y.shape, 1).astype(F32)).astype(BF16)
    source = jnp.concatenate([cells[k] for k in range(KC)], axis=1)
    held = jnp.dot(weight, source, preferred_element_type=F32)
    left = jnp.concatenate(
        [
            jnp.concatenate(
                [held[:, k * lanes + h * 128 : k * lanes + h * 128 + 128] for k in range(KC)],
                axis=1,
            )
            for h in range(halves)
        ],
        axis=0,
    ).astype(BF16)
    segments = TC // GRID
    position = 4 * iota((8, ccols), 1) + 1
    x = along(
        col_nodes(grids, g, c),
        position // GRID,
        c * TC + position,
        0.5,
        c * segments,
        segments,
        last_col(grids),
    )
    x = (x - 1.5) * 0.25
    pixels = [((c * KC + k) * coarse).astype(F32) for k in range(KC)]
    for k, slab, value in tap_fill(coarse, x, pixels):
        for s in range(half):
            at = k * 128 + s * coarse + 16 * slab
            spread[at : at + 16, s * ccols : (s + 1) * ccols] = value
    return jnp.dot(left, spread[...], preferred_element_type=F32)


def pan_piece(c, g, grids, cells, table):
    block = cells.shape[1] // KR
    position = iota((TR, 128), 0)
    y = along(row_nodes(grids, g), position // GRID, position, 0.0, 0, TR // GRID, TR // GRID - 1)
    lane = iota((TR, 128), 1)
    weight = jnp.concatenate(
        [
            cubic_weight(y - (lane + k * 128).astype(F32)).astype(BF16)
            for k in range(KR * block // 128)
        ],
        axis=1,
    )
    source = jnp.concatenate([cells[k] for k in range(KC)], axis=1)
    held = jnp.dot(weight, source, preferred_element_type=F32).astype(BF16)
    segments = TC // GRID
    v = iota((8, TC), 1)
    x = along(
        col_nodes(grids, g, c), v // GRID, c * TC + v, 0.0, c * segments, segments, last_col(grids)
    )
    pixels = [((c * KC + k) * block).astype(F32) for k in range(KC)]
    for k, slab, value in tap_fill(block, x, pixels):
        at = k * block + 16 * slab
        table[at : at + 16, :] = value
    return jnp.dot(held, table[...], preferred_element_type=F32)


def far_maps(n, bands, who, grids, ms_cells, pan_cells, *refs):
    pairs = n // 2
    outs, near = refs[:pairs], refs[pairs]
    spread, (table, edge) = refs[pairs + 1 : pairs + 3], refs[pairs + 3 :]
    step = pl.program_id(0)
    me, c = who[0], who[1]
    crows = TR // 4
    tall = crows + 8
    group = (8, TC)
    upper = iota(group, 0) < 4
    base = TR + 2 * crows

    @pl.when(step == 0)
    def _():
        for ref in spread:
            ref[...] = jnp.zeros_like(ref)

    mains = []
    for u in range(2):
        g = 2 * step + u
        ms_map = ms_piece(bands, c, g, grids, ms_cells[u], spread[u])
        main = jnp.concatenate([ms_map[0:crows], ms_map[tall : tall + crows]], axis=0)
        mains.append(main.astype(BF16))
        edge[(me ^ g) + 1] = jnp.where(upper, ms_map[crows:tall], ms_map[tall + crows : 2 * tall])
    pan_map = pan_piece(c, n - 1 - 2 * step, grids, pan_cells[0], table).astype(BF16)
    near[pairs - 1 - step, 0 : 2 * crows, :] = mains[0]
    for k in range(pairs):

        @pl.when(step == k)
        def _(k=k):
            outs[k][0:TR, :] = pan_map
            outs[pairs - 1 - k][TR:base, :] = mains[1]

    @pl.when(step == pairs - 1)
    def _():
        edge[0] = jnp.zeros(group, F32)
        edge[n + 1] = jnp.zeros(group, F32)
        mine = (iota(group, 0) & 2) == 0

        def halo(g):
            dest = me ^ g
            value = jnp.where(mine, edge[dest], edge[dest + 2])
            return jnp.concatenate([value, jnp.zeros_like(value)], axis=0).astype(BF16)

        for k in range(pairs):
            outs[k][base:, :] = halo(n - 1 - 2 * k)
            near[k, 2 * crows :, :] = halo(n - 2 - 2 * k)


def near_maps(n, fold, who, grids, ms, *refs):
    pairs = n // 2
    cells, outs, table = refs[:fold], refs[fold : fold + pairs], refs[fold + pairs :]
    step = pl.program_id(0)
    for u in range(fold):
        g = n - 2 - 2 * (fold * step + u)
        pan_map = pan_piece(who[1], g, grids, cells[u][0], table[u])
        ms_map = ms[u].astype(F32)
        for k in range(u, pairs, fold):

            @pl.when(fold * step + u == k)
            def _(k=k):
                outs[k][0:TR, :] = pan_map
                outs[k][TR:, :] = ms_map


def tables(bands, who, mix, gain, synth, up_out, cols_out):
    c = who[1]
    crows, ccols = TR // 4, TC // 4
    half = bands // 2
    v = iota((2 * ccols, TC), 1).astype(F32)
    q = iota((2 * ccols, TC), 0)
    q = jnp.where(q < ccols, q, jnp.where(c == 0, q, q - 2 * ccols)).astype(F32)
    cols_out[...] = cubic_weight((v - 1.5) * 0.25 - q).astype(BF16)
    lanes = up_out.shape[2]
    lane = iota((1, lanes), 1)
    s = lane // 80
    q = lane - s * 80
    e = q - 2 * crows
    low = q < 2 * crows
    h = jnp.where(low, q // crows, e // 4)
    band = jnp.where((s < half) & (q < 2 * crows + 8), h * half + s, -1)
    tail = e % 4
    w = jnp.where(low, 2 + q % crows, jnp.where(tail < 2, tail, crows + tail))
    r = iota((TR, lanes), 0).astype(F32)
    up = cubic_weight((r - 1.5) * 0.25 + 2.0 - w.astype(F32)).astype(BF16).astype(F32)
    for b in range(bands):
        factor = jnp.zeros((1, lanes), F32)
        for k in range(bands):
            value = mix[b, k] - gain[b] * synth[k]
            if k == b:
                value = value + 1.0
            factor = jnp.where(band == k, value, factor)
        up_out[b] = (up * factor).astype(BF16)


def finish(bands, gain, up_ref, cols_ref, ms_ref, other_ref, *refs):
    parts, (out, across, pan) = refs[:-3], refs[-3:]
    half = bands // 2
    ccols = TC // 4
    step = pl.program_id(0)

    @pl.when(step == 0)
    def _():
        pieces = []
        for s in range(half):
            at = slice(s * ccols, (s + 1) * ccols)
            pieces.append(jnp.concatenate([ms_ref[:, at], other_ref[:, at]], axis=1))
        left = jnp.concatenate(pieces, axis=0)
        rows = left.shape[0]
        across[0:rows, :] = jnp.dot(left, cols_ref[...], preferred_element_type=F32).astype(BF16)
        across[rows:, :] = jnp.zeros((across.shape[0] - rows, TC), BF16)
        total = parts[0][0:TR, :].astype(F32)
        for ref in parts[1:]:
            total = total + ref[0:TR, :].astype(F32)
        pan[...] = total

    count = up_ref.shape[0]
    for u in range(count):
        value = jnp.dot(up_ref[u], across[...], preferred_element_type=F32)
        out[u] = (value + gain[count * step + u] * pan[...]).astype(BF16)


def exchange(x, step, count):
    return lax.ppermute(x, "mrow", [(i, i ^ step) for i in range(count)])


def local(
    pan_blocks,
    ms_blocks,
    send_list,
    tile_list,
    row_grid,
    col_grid,
    band_mix,
    band_gain,
    synth_weight,
):
    n = lax.axis_size("mrow")
    me, c = lax.axis_index("mrow"), lax.axis_index("mcol")
    capacity = tile_list.shape[1] // n
    own, block = pan_blocks.shape[0], pan_blocks.shape[1]
    coarse = ms_blocks.shape[1]
    bands = band_gain.shape[0]
    who = jnp.stack([me, c]).astype(jnp.int32)

    other_cols = lax.ppermute(col_grid, "mcol", [(0, 1), (1, 0)])
    mine = jnp.concatenate([row_grid[None], col_grid, other_cols], axis=1)
    pair = jnp.concatenate([mine, exchange(mine, 1, n)], axis=0)
    grids = jnp.concatenate([pair] + [exchange(pair, k, n) for k in range(2, n, 2)], axis=0)

    group = min(n, 8)
    pan_cells, ms_cells = pl.pallas_call(
        functools.partial(cell_sums, group, capacity),
        grid=(n // group,),
        in_specs=[whole(pltpu.SMEM), whole(pltpu.SMEM), whole(), whole()],
        out_specs=[
            pl.BlockSpec((group * KC, KR * block, block), lambda i: (i, 0, 0)),
            pl.BlockSpec((group * KC, KR * coarse, bands * coarse), lambda i: (i, 0, 0)),
        ],
        out_shape=[
            jax.ShapeDtypeStruct((n * KC, KR * block, block), BF16),
            jax.ShapeDtypeStruct((n * KC, KR * coarse, bands * coarse), BF16),
        ],
        scratch_shapes=[
            pltpu.VMEM((group * KC, KR * block, block), F32),
            pltpu.VMEM((group * KC, KR * coarse, bands * coarse), F32),
        ],
        compiler_params=params(),
        name="cell_sums",
    )(who, send_list, pan_blocks, ms_blocks)

    start = TR
    tall = 2 * (TR // 4) + 16
    height = TR + tall
    pan_cells = pan_cells.reshape(n, KC, KR * block, block)
    ms_cells = ms_cells.reshape(n, KC, KR * coarse, bands * coarse)

    pairs = n // 2
    result = pl.BlockSpec((height, TC), lambda i: (0, 0))
    *far, near_ms = pl.pallas_call(
        functools.partial(far_maps, n, bands),
        grid=(pairs,),
        in_specs=[
            whole(pltpu.SMEM),
            whole(pltpu.SMEM),
            pl.BlockSpec((2,) + ms_cells.shape[1:], lambda i: (i, 0, 0, 0)),
            pl.BlockSpec((1,) + pan_cells.shape[1:], lambda i: (n - 1 - 2 * i, 0, 0, 0)),
        ],
        out_specs=[result] * pairs + [pl.BlockSpec((pairs, tall, TC), lambda i: (0, 0, 0))],
        scratch_shapes=[pltpu.VMEM((KC * 128, TC), BF16)] * 2
        + [pltpu.VMEM((KC * block, TC), BF16), pltpu.VMEM((n + 2, 8, TC), F32)],
        out_shape=[jax.ShapeDtypeStruct((height, TC), BF16)] * pairs
        + [jax.ShapeDtypeStruct((pairs, tall, TC), BF16)],
        compiler_params=params(),
        name="far_maps",
    )(who, grids, ms_cells, pan_cells)
    steps = [n - 2 - 2 * i for i in range(pairs)]
    theirs = [exchange(piece, 1, n) for piece in far]
    fold = 2
    near = pl.pallas_call(
        functools.partial(near_maps, n, fold),
        grid=(pairs // fold,),
        in_specs=[
            whole(pltpu.SMEM),
            whole(pltpu.SMEM),
            pl.BlockSpec((fold, tall, TC), lambda i: (i, 0, 0)),
        ]
        + [
            pl.BlockSpec(
                (1,) + pan_cells.shape[1:], lambda i, u=u: (n - 2 - 2 * (fold * i + u), 0, 0, 0)
            )
            for u in range(fold)
        ],
        out_specs=[result] * pairs,
        scratch_shapes=[pltpu.VMEM((KC * block, TC), BF16)] * fold,
        out_shape=[jax.ShapeDtypeStruct((height, TC), F32)] * pairs,
        compiler_params=params(),
        name="near_maps",
    )(who, grids, near_ms, *([pan_cells] * fold))

    lanes = 3 * 128
    up, cols = pl.pallas_call(
        functools.partial(tables, bands),
        in_specs=[whole(pltpu.SMEM)] * 4,
        out_specs=[whole(), whole()],
        out_shape=[
            jax.ShapeDtypeStruct((bands, TR, lanes), BF16),
            jax.ShapeDtypeStruct((TC // 2, TC), BF16),
        ],
        compiler_params=params(),
        name="tables",
    )(who, band_mix, band_gain, synth_weight)

    got = [near[-1], theirs[-1]]
    for k, a, b in zip(steps[:-1], near, theirs):
        got.append(exchange((a + b.astype(F32)).astype(BF16), k, n))
    ms_map = sum(part[start:].astype(F32) for part in got).astype(BF16)
    other = lax.ppermute(ms_map, "mcol", [(0, 1), (1, 0)])
    each = 2
    once = lambda x: pl.BlockSpec(x.shape, lambda i: (0, 0))
    return pl.pallas_call(
        functools.partial(finish, bands),
        grid=(bands // each,),
        in_specs=[
            whole(pltpu.SMEM),
            pl.BlockSpec((each, TR, lanes), lambda i: (i, 0, 0)),
            once(cols),
            once(ms_map),
            once(other),
        ]
        + [once(part) for part in got],
        out_specs=pl.BlockSpec((each, TR, TC), lambda i: (i, 0, 0)),
        out_shape=jax.ShapeDtypeStruct((bands, TR, TC), BF16),
        scratch_shapes=[pltpu.VMEM((lanes, TC), BF16), pltpu.VMEM((TR, TC), F32)],
        compiler_params=params(),
        name="finish",
    )(band_gain, up, cols, ms_map, other, *got)


def solution(mesh):
    return jax.shard_map(
        local,
        mesh=mesh,
        in_specs=(
            P(("scene", "mrow", "mcol"), None, None),
            P(("scene", "mrow", "mcol"), None, None),
            P(None, ("scene", "mrow", "mcol")),
            P(None, ("scene", "mrow", "mcol")),
            P(("scene", "mrow")),
            P(("scene", "mrow"), "mcol"),
            P(),
            P(),
            P(),
        ),
        out_specs=P(None, ("scene", "mrow"), "mcol"),
        check_vma=False,
    )
```

```python
import functools

import jax
import jax.numpy as jnp
from jax import lax
from jax.experimental import pallas as pl
from jax.experimental.pallas import tpu as pltpu
from jax.sharding import PartitionSpec as P

GRID = 64
TR = 128
TC = 512
KR = 2
KC = 5

F32 = jnp.float32
BF16 = jnp.bfloat16
MIB = 1024 * 1024


def params(mib):
    return pltpu.CompilerParams(vmem_limit_bytes=mib * MIB)


def whole(memory_space=pltpu.VMEM):
    return pl.BlockSpec(memory_space=memory_space)


def cubic_weight(offset):
    distance = jnp.abs(offset)
    near_part = (1.5 * distance - 2.5) * distance * distance + 1.0
    far_part = ((-0.5 * distance + 2.5) * distance - 4.0) * distance + 2.0
    return jnp.where(
        distance <= 1.0, near_part, jnp.where(distance < 2.0, far_part, jnp.zeros_like(distance))
    )


def iota(shape, dim):
    return lax.broadcasted_iota(jnp.int32, shape, dim)


def along(node, local, position, offset, first, count, last):
    left = jnp.zeros(position.shape, F32)
    right = left
    start = jnp.zeros(position.shape, jnp.int32)
    for k in range(count):
        segment = jnp.minimum(first + k, last)
        here = local == k
        left = jnp.where(here, node(segment), left)
        right = jnp.where(here, node(segment + 1), right)
        start = jnp.where(here, segment * GRID, start)
    within = ((position - start).astype(F32) + offset) / GRID
    return left + (right - left) * within


def repeat_rows(x):
    return jnp.concatenate([x, x], axis=0)


def tap_fill(rows, x, first_pixel):
    floor = jnp.floor(x)
    taps = [repeat_rows(cubic_weight(x - (floor - 1.0 + a))).astype(BF16) for a in range(4)]
    row = iota((16, x.shape[1]), 0).astype(F32)
    zero = jnp.zeros(row.shape, BF16)
    corner = floor - 1.0

    def at(first):
        offset = jnp.clip(corner - first, -8.0, rows + 8.0)
        base = (row - repeat_rows(offset)).astype(BF16)
        for slab in range(rows // 16):
            value = zero
            for a in range(4):
                value = jnp.where(base == jnp.asarray(a - 16 * slab, BF16), taps[a], value)
            yield slab, value

    for k, first in enumerate(first_pixel):
        for slab, value in at(first):
            yield k, slab, value


def row_nodes(grids, g):
    return lambda s: grids[g, s]


def col_nodes(grids, g, c):
    first = TR // GRID + 1
    each = (grids.shape[1] - first) // 2

    def node(s):
        half = s // each
        return grids[g, first + (half ^ c) * each + (s - half * each)]

    return node


def last_col(grids):
    return grids.shape[1] - (TR // GRID + 1) - 2


def ms_piece(bands, c, g, grids, cells, spread):
    coarse = cells[0].shape[0] // KR
    half = 128 // coarse
    halves = bands // half
    crows, ccols = TR // 4, TC // 4
    tall = crows + 8
    lanes = bands * coarse
    i = iota((tall, KR * coarse), 0)
    extra = (i - crows) % 4
    i = jnp.where(i < crows, i, jnp.where(extra < 2, crows - 2 + extra, extra - 2))
    position = 4 * i + 1
    y = along(row_nodes(grids, g), position // GRID, position, 0.5, 0, TR // GRID, TR // GRID - 1)
    y = (y - 1.5) * 0.25
    weight = cubic_weight(y - iota(y.shape, 1).astype(F32)).astype(BF16)
    source = jnp.concatenate([cells[k] for k in range(KC)], axis=1)
    held = jnp.dot(weight, source, preferred_element_type=F32)
    left = jnp.concatenate(
        [
            jnp.concatenate(
                [held[:, k * lanes + h * 128 : k * lanes + h * 128 + 128] for k in range(KC)],
                axis=1,
            )
            for h in range(halves)
        ],
        axis=0,
    ).astype(BF16)
    segments = TC // GRID
    position = 4 * iota((8, ccols), 1) + 1
    x = along(
        col_nodes(grids, g, c),
        position // GRID,
        c * TC + position,
        0.5,
        c * segments,
        segments,
        last_col(grids),
    )
    x = (x - 1.5) * 0.25
    pixels = [((c * KC + k) * coarse).astype(F32) for k in range(KC)]
    for k, slab, value in tap_fill(coarse, x, pixels):
        for s in range(half):
            at = k * 128 + s * coarse + 16 * slab
            spread[at : at + 16, s * ccols : (s + 1) * ccols] = value
    return jnp.dot(left, spread[...], preferred_element_type=F32)


def pan_piece(c, g, grids, cells, table):
    block = cells[0].shape[0] // KR
    position = iota((TR, 128), 0)
    y = along(row_nodes(grids, g), position // GRID, position, 0.0, 0, TR // GRID, TR // GRID - 1)
    lane = iota((TR, 128), 1)
    weight = jnp.concatenate(
        [
            cubic_weight(y - (lane + k * 128).astype(F32)).astype(BF16)
            for k in range(KR * block // 128)
        ],
        axis=1,
    )
    source = jnp.concatenate([cells[k] for k in range(KC)], axis=1)
    held = jnp.dot(weight, source, preferred_element_type=F32).astype(BF16)
    segments = TC // GRID
    v = iota((8, TC), 1)
    x = along(
        col_nodes(grids, g, c), v // GRID, c * TC + v, 0.0, c * segments, segments, last_col(grids)
    )
    pixels = [((c * KC + k) * block).astype(F32) for k in range(KC)]
    for k, slab, value in tap_fill(block, x, pixels):
        at = k * block + 16 * slab
        table[at : at + 16, :] = value
    return jnp.dot(held, table[...], preferred_element_type=F32)


def cell_sums(capacity, who, list_ref, pan_hbm, ms_hbm, pan_out, ms_out, *rest):
    pan_acc, ms_acc, pan_ref, ms_ref, sems = rest
    block, coarse = pan_ref.shape[1], ms_ref.shape[1]
    parts = sems.shape[0]
    each = pan_ref.shape[0] // parts
    copies = []
    for i in range(parts):
        at = pl.ds(i * each, each)
        copies.append(pltpu.make_async_copy(pan_hbm.at[at], pan_ref.at[at], sems.at[i, 0]))
        copies.append(pltpu.make_async_copy(ms_hbm.at[at], ms_ref.at[at], sems.at[i, 1]))
    for copy in copies:
        copy.start()
    pan_acc[...] = jnp.zeros_like(pan_acc)
    ms_acc[...] = jnp.zeros_like(ms_acc)

    def add(j, carry):
        place = (list_ref[0, j] // capacity) ^ who[0]
        row, col = list_ref[1, j], list_ref[2, j]
        cell = place * KC + lax.rem(col, KC)
        rows = pl.ds(pl.multiple_of(row * block, block), block)
        pan_acc[cell, rows, :] += pan_ref[j].astype(F32)
        rows = pl.ds(pl.multiple_of(row * coarse, coarse), coarse)
        ms_acc[cell, rows, :] += ms_ref[j].astype(F32)
        return carry

    for i in range(parts):
        copies[2 * i].wait()
        copies[2 * i + 1].wait()
        lax.fori_loop(i * each, (i + 1) * each, add, 0)
    pan_out[...] = pan_acc[...].astype(BF16)
    ms_out[...] = ms_acc[...].astype(BF16)


def halo_rows(above, below):
    mine = (iota(above.shape, 0) & 2) == 0
    value = jnp.where(mine, above, below)
    return jnp.concatenate([value, jnp.zeros_like(value)], axis=0).astype(BF16)


def ms_parts_of(ms_map):
    crows = TR // 4
    tall = crows + 8
    main = jnp.concatenate([ms_map[0:crows], ms_map[tall : tall + crows]], axis=0).astype(BF16)
    upper = iota((8, ms_map.shape[1]), 0) < 4
    return main, jnp.where(upper, ms_map[crows:tall], ms_map[tall + crows : 2 * tall])


def group_maps(n, bands, first, count, who, grids, cells_hbm, ms_hbm, *refs):
    scratch = refs[-7:]
    outs = refs[-7 - count : -7]
    spread, table, main, edge, cells, ms, sems = scratch
    me, c = who[0], who[1]
    low = (me ^ first) & -count
    around = [low + i for i in range(count)]
    around += [jnp.maximum(low - 1, 0), jnp.minimum(low + count, n - 1)]
    copies = [
        pltpu.make_async_copy(ms_hbm.at[pl.ds((t ^ me) * KC, KC)], ms.at[i], sems.at[i])
        for i, t in enumerate(around)
    ]
    copies.append(
        pltpu.make_async_copy(cells_hbm.at[pl.ds(first * KC, count * KC)], cells, sems.at[count + 2])
    )
    for copy in copies:
        copy.start()
    for ref in spread:
        ref[...] = jnp.zeros_like(ref)
    for copy in copies:
        copy.wait()
    for i, t in enumerate(around):
        held = [ms[i, j] for j in range(KC)]
        own, ends = ms_parts_of(ms_piece(bands, c, t ^ me, grids, held, spread[i % len(spread)]))
        if i < count:
            main[i] = own
            edge[i + 1] = ends
        elif i == count:
            edge[0] = jnp.where(low > 0, ends, jnp.zeros_like(ends))
        else:
            edge[count + 1] = jnp.where(low + count < n, ends, jnp.zeros_like(ends))
    base = TR + main.shape[1]
    for u in range(count):
        g = first + count - 1 - u
        held = [cells[(g - first) * KC + j] for j in range(KC)]
        out = outs[u]
        at = (me ^ g) - low
        out[0:TR, :] = pan_piece(c, g, grids, held, table[u]).astype(out.dtype)
        out[TR:base, :] = main[at].astype(out.dtype)
        out[base:, :] = halo_rows(edge[at], edge[at + 2]).astype(out.dtype)


def tables(bands, who, mix, gain, synth, after, up_out, cols_out):
    c = who[1]
    crows, ccols = TR // 4, TC // 4
    half = bands // 2
    v = iota((2 * ccols, TC), 1).astype(F32)
    q = iota((2 * ccols, TC), 0)
    q = jnp.where(q < ccols, q, jnp.where(c == 0, q, q - 2 * ccols)).astype(F32)
    cols_out[...] = cubic_weight((v - 1.5) * 0.25 - q).astype(BF16)
    lanes = up_out.shape[2]
    lane = iota((1, lanes), 1)
    s = lane // 80
    q = lane - s * 80
    e = q - 2 * crows
    low = q < 2 * crows
    h = jnp.where(low, q // crows, e // 4)
    band = jnp.where((s < half) & (q < 2 * crows + 8), h * half + s, -1)
    tail = e % 4
    w = jnp.where(low, 2 + q % crows, jnp.where(tail < 2, tail, crows + tail))
    r = iota((TR, lanes), 0).astype(F32)
    up = cubic_weight((r - 1.5) * 0.25 + 2.0 - w.astype(F32)).astype(BF16).astype(F32)
    for b in range(bands):
        factor = jnp.zeros((1, lanes), F32)
        for k in range(bands):
            value = mix[b, k] - gain[b] * synth[k]
            if k == b:
                value = value + 1.0
            factor = jnp.where(band == k, value, factor)
        up_out[b] = (up * factor).astype(BF16)


def finish(bands, gain, up_ref, cols_ref, ms_ref, other_ref, *refs):
    parts, (out, across, pan) = refs[:-3], refs[-3:]
    half = bands // 2
    ccols = TC // 4
    step = pl.program_id(0)

    @pl.when(step == 0)
    def _():
        pieces = []
        for s in range(half):
            at = slice(s * ccols, (s + 1) * ccols)
            pieces.append(jnp.concatenate([ms_ref[:, at], other_ref[:, at]], axis=1))
        left = jnp.concatenate(pieces, axis=0)
        rows = left.shape[0]
        across[0:rows, :] = jnp.dot(left, cols_ref[...], preferred_element_type=F32).astype(BF16)
        across[rows:, :] = jnp.zeros((across.shape[0] - rows, TC), BF16)
        total = parts[0][0:TR, :].astype(F32)
        for ref in parts[1:]:
            total = total + ref[0:TR, :].astype(F32)
        pan[...] = total

    count = up_ref.shape[0]
    table = jnp.concatenate([up_ref[u] for u in range(count)], axis=0)
    value = jnp.dot(table, across[...], preferred_element_type=F32)
    for u in range(count):
        band = value[u * TR : (u + 1) * TR]
        out[u] = (band + gain[count * step + u] * pan[...]).astype(BF16)


def exchange(x, step, count):
    return lax.ppermute(x, "mrow", [(i, i ^ step) for i in range(count)])


def local(
    pan_blocks,
    ms_blocks,
    send_list,
    tile_list,
    row_grid,
    col_grid,
    band_mix,
    band_gain,
    synth_weight,
):
    n = lax.axis_size("mrow")
    me, c = lax.axis_index("mrow"), lax.axis_index("mcol")
    capacity = tile_list.shape[1] // n
    own, block = pan_blocks.shape[0], pan_blocks.shape[1]
    coarse = ms_blocks.shape[1]
    bands = band_gain.shape[0]
    who = jnp.stack([me, c]).astype(jnp.int32)

    other_cols = lax.ppermute(col_grid, "mcol", [(0, 1), (1, 0)])
    mine = jnp.concatenate([row_grid[None], col_grid, other_cols], axis=1)
    pair = jnp.concatenate([mine, exchange(mine, 1, n)], axis=0)
    grids = jnp.concatenate([pair] + [exchange(pair, k, n) for k in range(2, n, 2)], axis=0)

    tall = 2 * (TR // 4) + 16
    height = TR + tall
    parts = 4
    hbm = pl.BlockSpec(memory_space=pltpu.HBM)
    cells, ms_cells = pl.pallas_call(
        functools.partial(cell_sums, capacity),
        in_specs=[whole(pltpu.SMEM)] * 2 + [hbm, hbm],
        out_specs=[whole()] * 2,
        out_shape=[
            jax.ShapeDtypeStruct((n * KC, KR * block, block), BF16),
            jax.ShapeDtypeStruct((n * KC, KR * coarse, bands * coarse), BF16),
        ],
        scratch_shapes=[
            pltpu.VMEM((n * KC, KR * block, block), F32),
            pltpu.VMEM((n * KC, KR * coarse, bands * coarse), F32),
            pltpu.VMEM(pan_blocks.shape, BF16),
            pltpu.VMEM(ms_blocks.shape, BF16),
            pltpu.SemaphoreType.DMA((parts, 2)),
        ],
        compiler_params=params(60),
        cost_estimate=pl.CostEstimate(flops=10**9, bytes_accessed=16 * MIB, transcendentals=0),
        name="cell_sums",
    )(who, send_list, pan_blocks, ms_blocks)
    top = n // 2

    held = {}

    def make(first, count, *after):
        order = range(first + count - 1, first - 1, -1)
        kept = [k == 0 or (k >= top and k % 2 == 0) for k in order]
        made = pl.pallas_call(
            functools.partial(group_maps, n, bands, first, count),
            in_specs=[whole(pltpu.SMEM)] * 2
            + [hbm] * 2
            + [pl.BlockSpec(memory_space=pl.ANY)] * len(after),
            out_specs=[whole()] * count,
            out_shape=[jax.ShapeDtypeStruct((height, TC), F32 if keep else BF16) for keep in kept],
            scratch_shapes=[
                [pltpu.VMEM((KC * 128, TC), BF16)] * 2,
                [pltpu.VMEM((KC * block, TC), BF16)] * count,
                pltpu.VMEM((count, tall - 16, TC), BF16),
                pltpu.VMEM((count + 2, 8, TC), F32),
                pltpu.VMEM((count * KC, KR * block, block), BF16),
                pltpu.VMEM((count + 2, KC, KR * coarse, bands * coarse), BF16),
                pltpu.SemaphoreType.DMA((count + 3,)),
            ],
            compiler_params=params(60),
            name="group_maps",
        )(who, grids, cells, ms_cells, *after)
        held.update((k, [piece]) for k, piece in zip(order, made))


    def pass_on(k, bit):
        got = held.pop(k)
        if len(got) > 1:
            got = [sum(part.astype(F32) for part in got).astype(BF16)]
        held[k ^ bit].append(exchange(got[0], bit, n))
        return got[0]

    after = ()
    for k in range(n - 2, top - 1, -2):
        make(k, 2, *after)
        after = (held[k + 1][0],)
    for k in range(n - 1, top - 1, -2):
        pass_on(k, 1)
    quad = min(4, top)
    bit = 2
    while bit < top:
        for k in range(n - bit, top - 1, -2 * bit):
            sent = pass_on(k, bit)
            if k == n - 2:
                for first in range(top - quad, -1, -quad):
                    make(first, quad, sent)
        bit *= 2
    filler = pass_on(top, top)
    for k in sorted(range(1, top), key=lambda k: -k):
        pass_on(k, k)
    mine, last, *others, early = held[0]
    got = [mine + early.astype(F32), *others, last]

    lanes = 3 * 128
    up, cols = pl.pallas_call(
        functools.partial(tables, bands),
        in_specs=[whole(pltpu.SMEM)] * 4 + [pl.BlockSpec(memory_space=pl.ANY)],
        out_specs=[whole(), whole()],
        out_shape=[
            jax.ShapeDtypeStruct((bands, TR, lanes), BF16),
            jax.ShapeDtypeStruct((TC // 2, TC), BF16),
        ],
        compiler_params=params(8),
        name="tables",
    )(who, band_mix, band_gain, synth_weight, filler)

    got, up, cols = lax.optimization_barrier((got, up, cols))
    ms_map = sum(part[TR:].astype(F32) for part in got).astype(BF16)
    other = lax.ppermute(ms_map, "mcol", [(0, 1), (1, 0)])
    each = 2
    once = lambda x: pl.BlockSpec(x.shape, lambda i: (0, 0))
    return pl.pallas_call(
        functools.partial(finish, bands),
        grid=(bands // each,),
        in_specs=[
            whole(pltpu.SMEM),
            pl.BlockSpec((each, TR, lanes), lambda i: (i, 0, 0)),
            once(cols),
            once(ms_map),
            once(other),
        ]
        + [once(part) for part in got],
        out_specs=pl.BlockSpec((each, TR, TC), lambda i: (i, 0, 0)),
        out_shape=jax.ShapeDtypeStruct((bands, TR, TC), BF16),
        scratch_shapes=[pltpu.VMEM((lanes, TC), BF16), pltpu.VMEM((TR, TC), F32)],
        compiler_params=params(16),
        name="finish",
    )(band_gain, up, cols, ms_map, other, *got)


def solution(mesh):
    return jax.shard_map(
        local,
        mesh=mesh,
        in_specs=(
            P(("scene", "mrow", "mcol"), None, None),
            P(("scene", "mrow", "mcol"), None, None),
            P(None, ("scene", "mrow", "mcol")),
            P(None, ("scene", "mrow", "mcol")),
            P(("scene", "mrow")),
            P(("scene", "mrow"), "mcol"),
            P(),
            P(),
            P(),
        ),
        out_specs=P(None, ("scene", "mrow"), "mcol"),
        check_vma=False,
    )
```

```python
import functools

import jax
import jax.numpy as jnp
from jax import lax
from jax.experimental import pallas as pl
from jax.experimental.pallas import tpu as pltpu
from jax.sharding import PartitionSpec as P

GRID = 64
TR = 128
TC = 512
KR = 2
KC = 5

F32 = jnp.float32
BF16 = jnp.bfloat16
MIB = 1024 * 1024


def params(mib):
    return pltpu.CompilerParams(vmem_limit_bytes=mib * MIB)


def whole(memory_space=pltpu.VMEM):
    return pl.BlockSpec(memory_space=memory_space)


def cubic_weight(offset):
    distance = jnp.abs(offset)
    near_part = (1.5 * distance - 2.5) * distance * distance + 1.0
    far_part = ((-0.5 * distance + 2.5) * distance - 4.0) * distance + 2.0
    return jnp.where(
        distance <= 1.0, near_part, jnp.where(distance < 2.0, far_part, jnp.zeros_like(distance))
    )


def iota(shape, dim):
    return lax.broadcasted_iota(jnp.int32, shape, dim)


def along(node, local, position, offset, first, count, last):
    left = jnp.zeros(position.shape, F32)
    right = left
    start = jnp.zeros(position.shape, jnp.int32)
    for k in range(count):
        segment = jnp.minimum(first + k, last)
        here = local == k
        left = jnp.where(here, node(segment), left)
        right = jnp.where(here, node(segment + 1), right)
        start = jnp.where(here, segment * GRID, start)
    within = ((position - start).astype(F32) + offset) / GRID
    return left + (right - left) * within


def repeat_rows(x):
    return jnp.concatenate([x, x], axis=0)


def tap_fill(rows, x, first_pixel):
    floor = jnp.floor(x)
    taps = [repeat_rows(cubic_weight(x - (floor - 1.0 + a))).astype(BF16) for a in range(4)]
    row = iota((16, x.shape[1]), 0).astype(F32)
    zero = jnp.zeros(row.shape, BF16)
    corner = floor - 1.0

    def at(first):
        offset = jnp.clip(corner - first, -8.0, rows + 8.0)
        base = (row - repeat_rows(offset)).astype(BF16)
        for slab in range(rows // 16):
            value = zero
            for a in range(4):
                value = jnp.where(base == jnp.asarray(a - 16 * slab, BF16), taps[a], value)
            yield slab, value

    for k, first in enumerate(first_pixel):
        for slab, value in at(first):
            yield k, slab, value


def row_nodes(grids, g):
    return lambda s: grids[g, s]


def col_nodes(grids, g, c):
    first = TR // GRID + 1
    each = (grids.shape[1] - first) // 2

    def node(s):
        half = s // each
        return grids[g, first + (half ^ c) * each + (s - half * each)]

    return node


def last_col(grids):
    return grids.shape[1] - (TR // GRID + 1) - 2


def ms_piece(bands, c, g, grids, cells, spread):
    coarse = cells[0].shape[0] // KR
    half = 128 // coarse
    halves = bands // half
    crows, ccols = TR // 4, TC // 4
    tall = crows + 8
    lanes = bands * coarse
    i = iota((tall, KR * coarse), 0)
    extra = (i - crows) % 4
    i = jnp.where(i < crows, i, jnp.where(extra < 2, crows - 2 + extra, extra - 2))
    position = 4 * i + 1
    y = along(row_nodes(grids, g), position // GRID, position, 0.5, 0, TR // GRID, TR // GRID - 1)
    y = (y - 1.5) * 0.25
    weight = cubic_weight(y - iota(y.shape, 1).astype(F32)).astype(BF16)
    source = jnp.concatenate([cells[k] for k in range(KC)], axis=1)
    held = jnp.dot(weight, source, preferred_element_type=F32)
    left = jnp.concatenate(
        [
            jnp.concatenate(
                [held[:, k * lanes + h * 128 : k * lanes + h * 128 + 128] for k in range(KC)],
                axis=1,
            )
            for h in range(halves)
        ],
        axis=0,
    ).astype(BF16)
    segments = TC // GRID
    position = 4 * iota((8, ccols), 1) + 1
    x = along(
        col_nodes(grids, g, c),
        position // GRID,
        c * TC + position,
        0.5,
        c * segments,
        segments,
        last_col(grids),
    )
    x = (x - 1.5) * 0.25
    pixels = [((c * KC + k) * coarse).astype(F32) for k in range(KC)]
    for k, slab, value in tap_fill(coarse, x, pixels):
        for s in range(half):
            at = k * 128 + s * coarse + 16 * slab
            spread[at : at + 16, s * ccols : (s + 1) * ccols] = value
    return jnp.dot(left, spread[...], preferred_element_type=F32)


def pan_piece(c, g, grids, cells, table):
    block = cells[0].shape[0] // KR
    position = iota((TR, 128), 0)
    y = along(row_nodes(grids, g), position // GRID, position, 0.0, 0, TR // GRID, TR // GRID - 1)
    lane = iota((TR, 128), 1)
    weight = jnp.concatenate(
        [
            cubic_weight(y - (lane + k * 128).astype(F32)).astype(BF16)
            for k in range(KR * block // 128)
        ],
        axis=1,
    )
    source = jnp.concatenate([cells[k] for k in range(KC)], axis=1)
    held = jnp.dot(weight, source, preferred_element_type=F32).astype(BF16)
    segments = TC // GRID
    v = iota((8, TC), 1)
    x = along(
        col_nodes(grids, g, c), v // GRID, c * TC + v, 0.0, c * segments, segments, last_col(grids)
    )
    pixels = [((c * KC + k) * block).astype(F32) for k in range(KC)]
    for k, slab, value in tap_fill(block, x, pixels):
        at = k * block + 16 * slab
        table[at : at + 16, :] = value
    return jnp.dot(held, table[...], preferred_element_type=F32)


def cell_sums(capacity, who, list_ref, pan_hbm, ms_hbm, pan_out, ms_out, *rest):
    pan_acc, ms_acc, pan_ref, ms_ref, sems = rest
    block, coarse = pan_ref.shape[1], ms_ref.shape[1]
    parts = sems.shape[0]
    each = pan_ref.shape[0] // parts
    copies = []
    for i in range(parts):
        at = pl.ds(i * each, each)
        copies.append(pltpu.make_async_copy(pan_hbm.at[at], pan_ref.at[at], sems.at[i, 0]))
        copies.append(pltpu.make_async_copy(ms_hbm.at[at], ms_ref.at[at], sems.at[i, 1]))
    for copy in copies:
        copy.start()
    pan_acc[...] = jnp.zeros_like(pan_acc)
    ms_acc[...] = jnp.zeros_like(ms_acc)

    def add(j, carry):
        place = (list_ref[0, j] // capacity) ^ who[0]
        row, col = list_ref[1, j], list_ref[2, j]
        cell = place * KC + lax.rem(col, KC)
        rows = pl.ds(pl.multiple_of(row * block, block), block)
        pan_acc[cell, rows, :] += pan_ref[j].astype(F32)
        rows = pl.ds(pl.multiple_of(row * coarse, coarse), coarse)
        ms_acc[cell, rows, :] += ms_ref[j].astype(F32)
        return carry

    for i in range(parts):
        copies[2 * i].wait()
        copies[2 * i + 1].wait()
        lax.fori_loop(i * each, (i + 1) * each, add, 0)
    pan_out[...] = pan_acc[...].astype(BF16)
    ms_out[...] = ms_acc[...].astype(BF16)


def halo_rows(above, below):
    mine = (iota(above.shape, 0) & 2) == 0
    value = jnp.where(mine, above, below)
    return jnp.concatenate([value, jnp.zeros_like(value)], axis=0).astype(BF16)


def ms_parts_of(ms_map):
    crows = TR // 4
    tall = crows + 8
    main = jnp.concatenate([ms_map[0:crows], ms_map[tall : tall + crows]], axis=0).astype(BF16)
    upper = iota((8, ms_map.shape[1]), 0) < 4
    return main, jnp.where(upper, ms_map[crows:tall], ms_map[tall + crows : 2 * tall])


def group_maps(n, bands, first, count, who, grids, cells_hbm, ms_hbm, *refs):
    scratch = refs[-7:]
    outs = refs[-7 - count : -7]
    spread, table, main, edge, cells, ms, sems = scratch
    me, c = who[0], who[1]
    low = (me ^ first) & -count
    around = [low + i for i in range(count)]
    around += [jnp.maximum(low - 1, 0), jnp.minimum(low + count, n - 1)]
    copies = [
        pltpu.make_async_copy(ms_hbm.at[pl.ds((t ^ me) * KC, KC)], ms.at[i], sems.at[i])
        for i, t in enumerate(around)
    ]
    copies.append(
        pltpu.make_async_copy(cells_hbm.at[pl.ds(first * KC, count * KC)], cells, sems.at[count + 2])
    )
    for copy in copies:
        copy.start()
    for ref in spread:
        ref[...] = jnp.zeros_like(ref)
    for copy in copies:
        copy.wait()
    for i, t in enumerate(around):
        held = [ms[i, j] for j in range(KC)]
        own, ends = ms_parts_of(ms_piece(bands, c, t ^ me, grids, held, spread[i % len(spread)]))
        if i < count:
            main[i] = own
            edge[i + 1] = ends
        elif i == count:
            edge[0] = jnp.where(low > 0, ends, jnp.zeros_like(ends))
        else:
            edge[count + 1] = jnp.where(low + count < n, ends, jnp.zeros_like(ends))
    base = TR + main.shape[1]
    for u in range(count):
        g = first + count - 1 - u
        held = [cells[(g - first) * KC + j] for j in range(KC)]
        out = outs[u]
        at = (me ^ g) - low
        out[0:TR, :] = pan_piece(c, g, grids, held, table[u]).astype(out.dtype)
        out[TR:base, :] = main[at].astype(out.dtype)
        out[base:, :] = halo_rows(edge[at], edge[at + 2]).astype(out.dtype)


def tables(bands, who, mix, gain, synth, after, up_out, cols_out):
    c = who[1]
    crows, ccols = TR // 4, TC // 4
    half = bands // 2
    v = iota((2 * ccols, TC), 1).astype(F32)
    q = iota((2 * ccols, TC), 0)
    q = jnp.where(q < ccols, q, jnp.where(c == 0, q, q - 2 * ccols)).astype(F32)
    cols_out[...] = cubic_weight((v - 1.5) * 0.25 - q).astype(BF16)
    lanes = up_out.shape[2]
    lane = iota((1, lanes), 1)
    s = lane // 80
    q = lane - s * 80
    e = q - 2 * crows
    low = q < 2 * crows
    h = jnp.where(low, q // crows, e // 4)
    band = jnp.where((s < half) & (q < 2 * crows + 8), h * half + s, -1)
    tail = e % 4
    w = jnp.where(low, 2 + q % crows, jnp.where(tail < 2, tail, crows + tail))
    r = iota((TR, lanes), 0).astype(F32)
    up = cubic_weight((r - 1.5) * 0.25 + 2.0 - w.astype(F32)).astype(BF16).astype(F32)
    for b in range(bands):
        factor = jnp.zeros((1, lanes), F32)
        for k in range(bands):
            value = mix[b, k] - gain[b] * synth[k]
            if k == b:
                value = value + 1.0
            factor = jnp.where(band == k, value, factor)
        up_out[b] = (up * factor).astype(BF16)


def finish(bands, gain, up_ref, cols_ref, ms_ref, other_ref, *refs):
    parts, (out, across, pan) = refs[:-3], refs[-3:]
    half = bands // 2
    ccols = TC // 4
    step = pl.program_id(0)

    @pl.when(step == 0)
    def _():
        pieces = []
        for s in range(half):
            at = slice(s * ccols, (s + 1) * ccols)
            pieces.append(jnp.concatenate([ms_ref[:, at], other_ref[:, at]], axis=1))
        left = jnp.concatenate(pieces, axis=0)
        rows = left.shape[0]
        across[0:rows, :] = jnp.dot(left, cols_ref[...], preferred_element_type=F32).astype(BF16)
        across[rows:, :] = jnp.zeros((across.shape[0] - rows, TC), BF16)
        total = parts[0][0:TR, :].astype(F32)
        for ref in parts[1:]:
            total = total + ref[0:TR, :].astype(F32)
        pan[...] = total

    count = up_ref.shape[0]
    table = jnp.concatenate([up_ref[u] for u in range(count)], axis=0)
    value = jnp.dot(table, across[...], preferred_element_type=F32)
    for u in range(count):
        band = value[u * TR : (u + 1) * TR]
        out[u] = (band + gain[count * step + u] * pan[...]).astype(BF16)


def exchange(x, step, count):
    return lax.ppermute(x, "mrow", [(i, i ^ step) for i in range(count)])


def local(
    pan_blocks,
    ms_blocks,
    send_list,
    tile_list,
    row_grid,
    col_grid,
    band_mix,
    band_gain,
    synth_weight,
):
    n = lax.axis_size("mrow")
    me, c = lax.axis_index("mrow"), lax.axis_index("mcol")
    capacity = tile_list.shape[1] // n
    own, block = pan_blocks.shape[0], pan_blocks.shape[1]
    coarse = ms_blocks.shape[1]
    bands = band_gain.shape[0]
    who = jnp.stack([me, c]).astype(jnp.int32)

    other_cols = lax.ppermute(col_grid, "mcol", [(0, 1), (1, 0)])
    mine = jnp.concatenate([row_grid[None], col_grid, other_cols], axis=1)
    pair = jnp.concatenate([mine, exchange(mine, 1, n)], axis=0)
    grids = jnp.concatenate([pair] + [exchange(pair, k, n) for k in range(2, n, 2)], axis=0)

    tall = 2 * (TR // 4) + 16
    height = TR + tall
    parts = 4
    hbm = pl.BlockSpec(memory_space=pltpu.HBM)
    cells, ms_cells = pl.pallas_call(
        functools.partial(cell_sums, capacity),
        in_specs=[whole(pltpu.SMEM)] * 2 + [hbm, hbm],
        out_specs=[whole()] * 2,
        out_shape=[
            jax.ShapeDtypeStruct((n * KC, KR * block, block), BF16),
            jax.ShapeDtypeStruct((n * KC, KR * coarse, bands * coarse), BF16),
        ],
        scratch_shapes=[
            pltpu.VMEM((n * KC, KR * block, block), F32),
            pltpu.VMEM((n * KC, KR * coarse, bands * coarse), F32),
            pltpu.VMEM(pan_blocks.shape, BF16),
            pltpu.VMEM(ms_blocks.shape, BF16),
            pltpu.SemaphoreType.DMA((parts, 2)),
        ],
        compiler_params=params(60),
        cost_estimate=pl.CostEstimate(flops=10**9, bytes_accessed=16 * MIB, transcendentals=0),
        name="cell_sums",
    )(who, send_list, pan_blocks, ms_blocks)
    top = n // 2

    held = {}

    def make(first, count, *after):
        order = range(first + count - 1, first - 1, -1)
        kept = [k == 0 or (k >= top and k % 2 == 0) for k in order]
        made = pl.pallas_call(
            functools.partial(group_maps, n, bands, first, count),
            in_specs=[whole(pltpu.SMEM)] * 2
            + [hbm] * 2
            + [pl.BlockSpec(memory_space=pl.ANY)] * len(after),
            out_specs=[whole()] * count,
            out_shape=[jax.ShapeDtypeStruct((height, TC), F32 if keep else BF16) for keep in kept],
            scratch_shapes=[
                [pltpu.VMEM((KC * 128, TC), BF16)] * 2,
                [pltpu.VMEM((KC * block, TC), BF16)] * count,
                pltpu.VMEM((count, tall - 16, TC), BF16),
                pltpu.VMEM((count + 2, 8, TC), F32),
                pltpu.VMEM((count * KC, KR * block, block), BF16),
                pltpu.VMEM((count + 2, KC, KR * coarse, bands * coarse), BF16),
                pltpu.SemaphoreType.DMA((count + 3,)),
            ],
            compiler_params=params(60),
            name="group_maps",
        )(who, grids, cells, ms_cells, *after)
        held.update((k, [piece]) for k, piece in zip(order, made))


    def pass_on(k, bit):
        got = held.pop(k)
        if len(got) > 1:
            got = [sum(part.astype(F32) for part in got).astype(BF16)]
        held[k ^ bit].append(exchange(got[0], bit, n))
        return got[0]

    after = ()
    for k in range(n - 2, top - 1, -2):
        make(k, 2, *after)
        after = (held[k + 1][0],)
    for k in range(n - 1, top - 1, -2):
        pass_on(k, 1)
    quad = min(4, top)
    bit = 2
    while bit < top:
        for k in range(n - bit, top - 1, -2 * bit):
            sent = pass_on(k, bit)
            if k == n - 2:
                for first in range(top - quad, -1, -quad):
                    make(first, quad, sent)
        bit *= 2
    filler = pass_on(top, top)
    for k in sorted(range(1, top), key=lambda k: -k):
        pass_on(k, k)
    mine, last, *others, early = held[0]
    got = [mine + early.astype(F32), *others, last]

    lanes = 3 * 128
    up, cols = pl.pallas_call(
        functools.partial(tables, bands),
        in_specs=[whole(pltpu.SMEM)] * 4 + [pl.BlockSpec(memory_space=pl.ANY)],
        out_specs=[whole(), whole()],
        out_shape=[
            jax.ShapeDtypeStruct((bands, TR, lanes), BF16),
            jax.ShapeDtypeStruct((TC // 2, TC), BF16),
        ],
        compiler_params=params(8),
        name="tables",
    )(who, band_mix, band_gain, synth_weight, filler)

    got, up, cols = lax.optimization_barrier((got, up, cols))
    ms_map = sum(part[TR:].astype(F32) for part in got).astype(BF16)
    other = lax.ppermute(ms_map, "mcol", [(0, 1), (1, 0)])
    each = 4
    once = lambda x: pl.BlockSpec(x.shape, lambda i: (0, 0))
    return pl.pallas_call(
        functools.partial(finish, bands),
        grid=(bands // each,),
        in_specs=[
            whole(pltpu.SMEM),
            pl.BlockSpec((each, TR, lanes), lambda i: (i, 0, 0)),
            once(cols),
            once(ms_map),
            once(other),
        ]
        + [once(part) for part in got],
        out_specs=pl.BlockSpec((each, TR, TC), lambda i: (i, 0, 0)),
        out_shape=jax.ShapeDtypeStruct((bands, TR, TC), BF16),
        scratch_shapes=[pltpu.VMEM((lanes, TC), BF16), pltpu.VMEM((TR, TC), F32)],
        compiler_params=params(16),
        name="finish",
    )(band_gain, up, cols, ms_map, other, *got)


def solution(mesh):
    return jax.shard_map(
        local,
        mesh=mesh,
        in_specs=(
            P(("scene", "mrow", "mcol"), None, None),
            P(("scene", "mrow", "mcol"), None, None),
            P(None, ("scene", "mrow", "mcol")),
            P(None, ("scene", "mrow", "mcol")),
            P(("scene", "mrow")),
            P(("scene", "mrow"), "mcol"),
            P(),
            P(),
            P(),
        ),
        out_specs=P(None, ("scene", "mrow"), "mcol"),
        check_vma=False,
    )
```

```python
import functools

import jax
import jax.numpy as jnp
from jax import lax
from jax.experimental import pallas as pl
from jax.experimental.pallas import tpu as pltpu
from jax.sharding import PartitionSpec as P

GRID = 64
TR = 128
TC = 512
KR = 2
KC = 5

F32 = jnp.float32
BF16 = jnp.bfloat16
MIB = 1024 * 1024


def params(mib):
    return pltpu.CompilerParams(vmem_limit_bytes=mib * MIB)


def whole(memory_space=pltpu.VMEM):
    return pl.BlockSpec(memory_space=memory_space)


def cubic_weight(offset):
    distance = jnp.abs(offset)
    near_part = (1.5 * distance - 2.5) * distance * distance + 1.0
    far_part = ((-0.5 * distance + 2.5) * distance - 4.0) * distance + 2.0
    return jnp.where(
        distance <= 1.0, near_part, jnp.where(distance < 2.0, far_part, jnp.zeros_like(distance))
    )


def iota(shape, dim):
    return lax.broadcasted_iota(jnp.int32, shape, dim)


def along(node, local, position, offset, first, count, last):
    left = jnp.zeros(position.shape, F32)
    right = left
    start = jnp.zeros(position.shape, jnp.int32)
    for k in range(count):
        segment = jnp.minimum(first + k, last)
        here = local == k
        left = jnp.where(here, node(segment), left)
        right = jnp.where(here, node(segment + 1), right)
        start = jnp.where(here, segment * GRID, start)
    within = ((position - start).astype(F32) + offset) / GRID
    return left + (right - left) * within


def repeat_rows(x):
    return jnp.concatenate([x, x], axis=0)


def tap_fill(rows, x, first_pixel):
    floor = jnp.floor(x)
    taps = [repeat_rows(cubic_weight(x - (floor - 1.0 + a))).astype(BF16) for a in range(4)]
    row = iota((16, x.shape[1]), 0).astype(F32)
    zero = jnp.zeros(row.shape, BF16)
    corner = floor - 1.0

    def at(first):
        offset = jnp.clip(corner - first, -8.0, rows + 8.0)
        base = (row - repeat_rows(offset)).astype(BF16)
        for slab in range(rows // 16):
            value = zero
            for a in range(4):
                value = jnp.where(base == jnp.asarray(a - 16 * slab, BF16), taps[a], value)
            yield slab, value

    for k, first in enumerate(first_pixel):
        for slab, value in at(first):
            yield k, slab, value


def row_nodes(grids, g):
    return lambda s: grids[g, s]


def col_nodes(grids, g, c):
    first = TR // GRID + 1
    each = (grids.shape[1] - first) // 2

    def node(s):
        half = s // each
        return grids[g, first + (half ^ c) * each + (s - half * each)]

    return node


def last_col(grids):
    return grids.shape[1] - (TR // GRID + 1) - 2


def ms_piece(bands, c, g, grids, cells, spread):
    coarse = cells[0].shape[0] // KR
    half = 128 // coarse
    halves = bands // half
    crows, ccols = TR // 4, TC // 4
    tall = crows + 8
    lanes = bands * coarse
    i = iota((tall, KR * coarse), 0)
    extra = (i - crows) % 4
    i = jnp.where(i < crows, i, jnp.where(extra < 2, crows - 2 + extra, extra - 2))
    position = 4 * i + 1
    y = along(row_nodes(grids, g), position // GRID, position, 0.5, 0, TR // GRID, TR // GRID - 1)
    y = (y - 1.5) * 0.25
    weight = cubic_weight(y - iota(y.shape, 1).astype(F32)).astype(BF16)
    source = jnp.concatenate([cells[k] for k in range(KC)], axis=1)
    held = jnp.dot(weight, source, preferred_element_type=F32)
    left = jnp.concatenate(
        [
            jnp.concatenate(
                [held[:, k * lanes + h * 128 : k * lanes + h * 128 + 128] for k in range(KC)],
                axis=1,
            )
            for h in range(halves)
        ],
        axis=0,
    ).astype(BF16)
    segments = TC // GRID
    position = 4 * iota((8, ccols), 1) + 1
    x = along(
        col_nodes(grids, g, c),
        position // GRID,
        c * TC + position,
        0.5,
        c * segments,
        segments,
        last_col(grids),
    )
    x = (x - 1.5) * 0.25
    pixels = [((c * KC + k) * coarse).astype(F32) for k in range(KC)]
    for k, slab, value in tap_fill(coarse, x, pixels):
        for s in range(half):
            at = k * 128 + s * coarse + 16 * slab
            spread[at : at + 16, s * ccols : (s + 1) * ccols] = value
    return jnp.dot(left, spread[...], preferred_element_type=F32)


def pan_piece(c, g, grids, cells, table):
    block = cells[0].shape[0] // KR
    position = iota((TR, 128), 0)
    y = along(row_nodes(grids, g), position // GRID, position, 0.0, 0, TR // GRID, TR // GRID - 1)
    lane = iota((TR, 128), 1)
    weight = jnp.concatenate(
        [
            cubic_weight(y - (lane + k * 128).astype(F32)).astype(BF16)
            for k in range(KR * block // 128)
        ],
        axis=1,
    )
    source = jnp.concatenate([cells[k] for k in range(KC)], axis=1)
    held = jnp.dot(weight, source, preferred_element_type=F32).astype(BF16)
    segments = TC // GRID
    v = iota((8, TC), 1)
    x = along(
        col_nodes(grids, g, c), v // GRID, c * TC + v, 0.0, c * segments, segments, last_col(grids)
    )
    pixels = [((c * KC + k) * block).astype(F32) for k in range(KC)]
    for k, slab, value in tap_fill(block, x, pixels):
        at = k * block + 16 * slab
        table[at : at + 16, :] = value
    return jnp.dot(held, table[...], preferred_element_type=F32)


def cell_sums(capacity, who, list_ref, pan_hbm, ms_hbm, pan_out, ms_out, *rest):
    pan_acc, ms_acc, pan_ref, ms_ref, sems = rest
    block, coarse = pan_ref.shape[1], ms_ref.shape[1]
    parts = sems.shape[0]
    each = pan_ref.shape[0] // parts
    copies = []
    for i in range(parts):
        at = pl.ds(i * each, each)
        copies.append(pltpu.make_async_copy(pan_hbm.at[at], pan_ref.at[at], sems.at[i, 0]))
        copies.append(pltpu.make_async_copy(ms_hbm.at[at], ms_ref.at[at], sems.at[i, 1]))
    for copy in copies:
        copy.start()
    pan_acc[...] = jnp.zeros_like(pan_acc)
    ms_acc[...] = jnp.zeros_like(ms_acc)

    def add(j, carry):
        place = (list_ref[0, j] // capacity) ^ who[0]
        row, col = list_ref[1, j], list_ref[2, j]
        cell = place * KC + lax.rem(col, KC)
        rows = pl.ds(pl.multiple_of(row * block, block), block)
        pan_acc[cell, rows, :] += pan_ref[j].astype(F32)
        rows = pl.ds(pl.multiple_of(row * coarse, coarse), coarse)
        ms_acc[cell, rows, :] += ms_ref[j].astype(F32)
        return carry

    for i in range(parts):
        copies[2 * i].wait()
        copies[2 * i + 1].wait()
        lax.fori_loop(i * each, (i + 1) * each, add, 0)
    pan_out[...] = pan_acc[...].astype(BF16)
    ms_out[...] = ms_acc[...].astype(BF16)


def halo_rows(above, below):
    mine = (iota(above.shape, 0) & 2) == 0
    value = jnp.where(mine, above, below)
    return jnp.concatenate([value, jnp.zeros_like(value)], axis=0).astype(BF16)


def ms_parts_of(ms_map):
    crows = TR // 4
    tall = crows + 8
    main = jnp.concatenate([ms_map[0:crows], ms_map[tall : tall + crows]], axis=0).astype(BF16)
    upper = iota((8, ms_map.shape[1]), 0) < 4
    return main, jnp.where(upper, ms_map[crows:tall], ms_map[tall + crows : 2 * tall])


def group_maps(n, bands, first, count, who, grids, cells_hbm, ms_hbm, *refs):
    scratch = refs[-7:]
    outs = refs[-7 - count : -7]
    spread, table, main, edge, cells, ms, sems = scratch
    me, c = who[0], who[1]
    low = (me ^ first) & -count
    around = [low + i for i in range(count)]
    around += [jnp.maximum(low - 1, 0), jnp.minimum(low + count, n - 1)]
    copies = [
        pltpu.make_async_copy(ms_hbm.at[pl.ds((t ^ me) * KC, KC)], ms.at[i], sems.at[i])
        for i, t in enumerate(around)
    ]
    copies.append(
        pltpu.make_async_copy(cells_hbm.at[pl.ds(first * KC, count * KC)], cells, sems.at[count + 2])
    )
    for copy in copies:
        copy.start()
    for ref in spread:
        ref[...] = jnp.zeros_like(ref)
    for copy in copies:
        copy.wait()
    for i, t in enumerate(around):
        held = [ms[i, j] for j in range(KC)]
        own, ends = ms_parts_of(ms_piece(bands, c, t ^ me, grids, held, spread[i % len(spread)]))
        if i < count:
            main[i] = own
            edge[i + 1] = ends
        elif i == count:
            edge[0] = jnp.where(low > 0, ends, jnp.zeros_like(ends))
        else:
            edge[count + 1] = jnp.where(low + count < n, ends, jnp.zeros_like(ends))
    base = TR + main.shape[1]
    for u in range(count):
        g = first + count - 1 - u
        held = [cells[(g - first) * KC + j] for j in range(KC)]
        out = outs[u]
        at = (me ^ g) - low
        out[0:TR, :] = pan_piece(c, g, grids, held, table[u]).astype(out.dtype)
        out[TR:base, :] = main[at].astype(out.dtype)
        out[base:, :] = halo_rows(edge[at], edge[at + 2]).astype(out.dtype)


def tables(bands, who, mix, gain, synth, after, up_out, cols_out):
    c = who[1]
    crows, ccols = TR // 4, TC // 4
    half = bands // 2
    v = iota((2 * ccols, TC), 1).astype(F32)
    q = iota((2 * ccols, TC), 0)
    q = jnp.where(q < ccols, q, jnp.where(c == 0, q, q - 2 * ccols)).astype(F32)
    cols_out[...] = cubic_weight((v - 1.5) * 0.25 - q).astype(BF16)
    lanes = up_out.shape[2]
    lane = iota((1, lanes), 1)
    s = lane // 80
    q = lane - s * 80
    e = q - 2 * crows
    low = q < 2 * crows
    h = jnp.where(low, q // crows, e // 4)
    band = jnp.where((s < half) & (q < 2 * crows + 8), h * half + s, -1)
    tail = e % 4
    w = jnp.where(low, 2 + q % crows, jnp.where(tail < 2, tail, crows + tail))
    r = iota((TR, lanes), 0).astype(F32)
    up = cubic_weight((r - 1.5) * 0.25 + 2.0 - w.astype(F32)).astype(BF16).astype(F32)
    for b in range(bands):
        factor = jnp.zeros((1, lanes), F32)
        for k in range(bands):
            value = mix[b, k] - gain[b] * synth[k]
            if k == b:
                value = value + 1.0
            factor = jnp.where(band == k, value, factor)
        up_out[b] = (up * factor).astype(BF16)


def finish(bands, gain, up_ref, cols_ref, ms_ref, other_ref, *refs):
    parts, (out, across, pan) = refs[:-3], refs[-3:]
    half = bands // 2
    ccols = TC // 4
    step = pl.program_id(0)

    @pl.when(step == 0)
    def _():
        pieces = []
        for s in range(half):
            at = slice(s * ccols, (s + 1) * ccols)
            pieces.append(jnp.concatenate([ms_ref[:, at], other_ref[:, at]], axis=1))
        left = jnp.concatenate(pieces, axis=0)
        rows = left.shape[0]
        across[0:rows, :] = jnp.dot(left, cols_ref[...], preferred_element_type=F32).astype(BF16)
        across[rows:, :] = jnp.zeros((across.shape[0] - rows, TC), BF16)
        total = parts[0][0:TR, :].astype(F32)
        for ref in parts[1:]:
            total = total + ref[0:TR, :].astype(F32)
        pan[...] = total

    count = up_ref.shape[0]
    table = jnp.concatenate([up_ref[u] for u in range(count)], axis=0)
    value = jnp.dot(table, across[...], preferred_element_type=F32)
    for u in range(count):
        band = value[u * TR : (u + 1) * TR]
        out[u] = (band + gain[count * step + u] * pan[...]).astype(BF16)


def exchange(x, step, count):
    return lax.ppermute(x, "mrow", [(i, i ^ step) for i in range(count)])


def local(
    pan_blocks,
    ms_blocks,
    send_list,
    tile_list,
    row_grid,
    col_grid,
    band_mix,
    band_gain,
    synth_weight,
):
    n = lax.axis_size("mrow")
    me, c = lax.axis_index("mrow"), lax.axis_index("mcol")
    capacity = tile_list.shape[1] // n
    own, block = pan_blocks.shape[0], pan_blocks.shape[1]
    coarse = ms_blocks.shape[1]
    bands = band_gain.shape[0]
    who = jnp.stack([me, c]).astype(jnp.int32)

    other_cols = lax.ppermute(col_grid, "mcol", [(0, 1), (1, 0)])
    mine = jnp.concatenate([row_grid[None], col_grid, other_cols], axis=1)
    pair = jnp.concatenate([mine, exchange(mine, 1, n)], axis=0)
    grids = jnp.concatenate([pair] + [exchange(pair, k, n) for k in range(2, n, 2)], axis=0)

    tall = 2 * (TR // 4) + 16
    height = TR + tall
    parts = 4
    hbm = pl.BlockSpec(memory_space=pltpu.HBM)
    cells, ms_cells = pl.pallas_call(
        functools.partial(cell_sums, capacity),
        in_specs=[whole(pltpu.SMEM)] * 2 + [hbm, hbm],
        out_specs=[whole()] * 2,
        out_shape=[
            jax.ShapeDtypeStruct((n * KC, KR * block, block), BF16),
            jax.ShapeDtypeStruct((n * KC, KR * coarse, bands * coarse), BF16),
        ],
        scratch_shapes=[
            pltpu.VMEM((n * KC, KR * block, block), F32),
            pltpu.VMEM((n * KC, KR * coarse, bands * coarse), F32),
            pltpu.VMEM(pan_blocks.shape, BF16),
            pltpu.VMEM(ms_blocks.shape, BF16),
            pltpu.SemaphoreType.DMA((parts, 2)),
        ],
        compiler_params=params(60),
        cost_estimate=pl.CostEstimate(flops=10**9, bytes_accessed=16 * MIB, transcendentals=0),
        name="cell_sums",
    )(who, send_list, pan_blocks, ms_blocks)
    top = n // 2

    held = {}

    def make(first, count, *after):
        order = range(first + count - 1, first - 1, -1)
        kept = [k == 0 or (k >= top and k % 2 == 0) for k in order]
        made = pl.pallas_call(
            functools.partial(group_maps, n, bands, first, count),
            in_specs=[whole(pltpu.SMEM)] * 2
            + [hbm] * 2
            + [pl.BlockSpec(memory_space=pl.ANY)] * len(after),
            out_specs=[whole()] * count,
            out_shape=[jax.ShapeDtypeStruct((height, TC), F32 if keep else BF16) for keep in kept],
            scratch_shapes=[
                [pltpu.VMEM((KC * 128, TC), BF16)] * 2,
                [pltpu.VMEM((KC * block, TC), BF16)] * count,
                pltpu.VMEM((count, tall - 16, TC), BF16),
                pltpu.VMEM((count + 2, 8, TC), F32),
                pltpu.VMEM((count * KC, KR * block, block), BF16),
                pltpu.VMEM((count + 2, KC, KR * coarse, bands * coarse), BF16),
                pltpu.SemaphoreType.DMA((count + 3,)),
            ],
            compiler_params=params(44),
            name="group_maps",
        )(who, grids, cells, ms_cells, *after)
        held.update((k, [piece]) for k, piece in zip(order, made))


    def pass_on(k, bit):
        got = held.pop(k)
        if len(got) > 1:
            got = [sum(part.astype(F32) for part in got).astype(BF16)]
        held[k ^ bit].append(exchange(got[0], bit, n))
        return got[0]

    after = ()
    for k in range(n - 2, top - 1, -2):
        make(k, 2, *after)
        after = (held[k + 1][0],)
    for k in range(n - 1, top - 1, -2):
        pass_on(k, 1)
    quad = min(4, top)
    bit = 2
    while bit < top:
        for k in range(n - bit, top - 1, -2 * bit):
            sent = pass_on(k, bit)
            if k == n - 2:
                for first in range(top - quad, -1, -quad):
                    make(first, quad, sent)
        bit *= 2
    filler = pass_on(top, top)
    for k in sorted(range(1, top), key=lambda k: -k):
        pass_on(k, k)
    mine, last, *others, early = held[0]
    got = [mine + early.astype(F32), *others, last]

    lanes = 3 * 128
    up, cols = pl.pallas_call(
        functools.partial(tables, bands),
        in_specs=[whole(pltpu.SMEM)] * 4 + [pl.BlockSpec(memory_space=pl.ANY)],
        out_specs=[whole(), whole()],
        out_shape=[
            jax.ShapeDtypeStruct((bands, TR, lanes), BF16),
            jax.ShapeDtypeStruct((TC // 2, TC), BF16),
        ],
        compiler_params=params(8),
        name="tables",
    )(who, band_mix, band_gain, synth_weight, filler)

    got, up, cols = lax.optimization_barrier((got, up, cols))
    ms_map = sum(part[TR:].astype(F32) for part in got).astype(BF16)
    other = lax.ppermute(ms_map, "mcol", [(0, 1), (1, 0)])
    each = 4
    once = lambda x: pl.BlockSpec(x.shape, lambda i: (0, 0))
    return pl.pallas_call(
        functools.partial(finish, bands),
        grid=(bands // each,),
        in_specs=[
            whole(pltpu.SMEM),
            pl.BlockSpec((each, TR, lanes), lambda i: (i, 0, 0)),
            once(cols),
            once(ms_map),
            once(other),
        ]
        + [once(part) for part in got],
        out_specs=pl.BlockSpec((each, TR, TC), lambda i: (i, 0, 0)),
        out_shape=jax.ShapeDtypeStruct((bands, TR, TC), BF16),
        scratch_shapes=[pltpu.VMEM((lanes, TC), BF16), pltpu.VMEM((TR, TC), F32)],
        compiler_params=params(16),
        name="finish",
    )(band_gain, up, cols, ms_map, other, *got)


def solution(mesh):
    return jax.shard_map(
        local,
        mesh=mesh,
        in_specs=(
            P(("scene", "mrow", "mcol"), None, None),
            P(("scene", "mrow", "mcol"), None, None),
            P(None, ("scene", "mrow", "mcol")),
            P(None, ("scene", "mrow", "mcol")),
            P(("scene", "mrow")),
            P(("scene", "mrow"), "mcol"),
            P(),
            P(),
            P(),
        ),
        out_specs=P(None, ("scene", "mrow"), "mcol"),
        check_vma=False,
    )
```
